512 devices in a mesh: pipe: 32 (over z, core), tp: 16 (over x, y).
Axes of the slice: x: 4, y: 4, z: 16, core: 2. Of those that a mesh axis runs over, the one named last changes fastest.
Arguments:
- saved: bfloat16 [32, 2, 128, 4096], P('pipe', None, None, 'tp'), may hold values from -26 to 26
- incoming: bfloat16 [32, 128, 4096], P('pipe', None, 'tp'), may hold values from -6 to 6
- gain: bfloat16 [32, 4096], P('pipe'), may hold values from 0.5 to 1.5
- w_query: bfloat16 [32, 4096, 4096], P('pipe', None, 'tp'), may hold values from -0.09375 to 0.09375
- w_key: bfloat16 [32, 4096, 512], P('pipe', None, 'tp'), may hold values from -0.09375 to 0.09375
- w_value: bfloat16 [32, 4096, 512], P('pipe', None, 'tp'), may hold values from -0.09375 to 0.09375
- w_out: bfloat16 [32, 4096, 4096], P('pipe', 'tp'), may hold values from -0.09375 to 0.09375
- seg_lengths: int32 [32, 2, 4], P('pipe'), may hold values from 1 to 64, 128 in all within a row
- score_grad: bfloat16 [2, 128, 4096], P(None, None, 'tp'), may hold values from -6 to 6
- rewards: float32 [512], replicated, may hold values from -3 to 3
- sample_group: int32 [512], replicated, may hold values from 0 to 31, as said below
- head_sample: int32 [2, 128], replicated, may hold values from 0 to 511
Outputs:
- emitted: bfloat16 [32, 2, 128, 4096], P('pipe', None, None, 'tp')
- carried: bfloat16 [32, 128, 4096], P('pipe', None, 'tp')
The draws below stay inside these ranges and needn't reach their ends.
Inputs may be any that keep to these rules, and one draw needn't show every extreme that they name: `sample_group`: each of the 32 prompt ids names exactly 16 rollouts.
All inputs are finite; a program needn't handle non-finite values.
Results may differ from the reference program's by a relative error of at most 0.027.
Values may be sent and summed in bfloat16 or wider, within the bound.
No kernel may reach another device: no remote copies, remote signals or barrier semaphores. Data moves between devices by JAX's collectives and lax.ppermute only.
A program may use at most 64 MiB of HBM per device.

```python
import math
import jax
import jax.numpy as jnp
import numpy as np
from jax import lax

D = 4096
HEADS = 32
KV = 4
HD = 128
ROWS = 128
TICKS = 2
SEGS = 4
MOST_SEG = 64
SAMPLES = 512
GROUP_SIZE = 16
GROUPS = 32
SECTIONS = 32
N_TP = 16


def draw_saved(key, part):
    key = jax.random.fold_in(key, 7)
    base_key, row_key = jax.random.split(key)
    full_shape = (SECTIONS, TICKS, ROWS, D)
    column_ramp = jnp.arange(D, dtype=jnp.float32) / (D - 1)
    base_values = jnp.clip(jax.random.normal(base_key, full_shape, jnp.float32), -4.0, 4.0)
    column = jnp.exp(column_ramp * math.log(10.0)) / math.sqrt(99.0 / (2.0 * math.log(10.0)))
    row_log = jax.random.uniform(row_key, (SECTIONS, TICKS, ROWS, 1), jnp.float32, math.log(0.3), math.log(3.0))
    return (base_values * column[None, None, None, :] * jnp.exp(row_log)).astype(jnp.bfloat16)


def draw_sample_group(key, part):
    key = jax.random.fold_in(key, 19)
    ordering = jax.random.permutation(key, SAMPLES)
    return (ordering // GROUP_SIZE).astype(jnp.int32)


def plant(array, rng, low, top_value):
    longest = array.shape.index(max(array.shape))
    spots = []
    for shift in (0, 1):
        where = [jax.random.randint(jax.random.fold_in(rng, axis), (), 0, length) for axis, length in enumerate(array.shape)]
        where[longest] = (where[longest] + shift) % array.shape[longest]
        spots.append(tuple(where))
    return array.at[spots[0]].set(low).at[spots[1]].set(top_value)


def shard_levels(key, shape, cuts, least, top_value):
    level, own = 1.0, jax.random.fold_in(key, 6)
    for dim, shards_of in cuts:
        heights = jnp.exp(jax.random.uniform(jax.random.fold_in(own, dim), (shards_of,), jnp.float32, least / len(cuts), top_value / len(cuts)))
        level = level * jnp.repeat(heights, shape[dim] // shards_of).reshape([-1 if axis == dim else 1 for axis in range(len(shape))])
    return level


def split_up(count, total, bound, lean):
    loads = [(1 << 20) // math.isqrt(standing ** lean) + 1 for standing in range(2, count + 1)]
    surplus, given = total - bound - (count - 1), [1] * (count - 1)
    while surplus > 0:
        candidates = [i for i in range(count - 1) if given[i] < bound]
        whole, budget = sum([loads[i] for i in candidates]), surplus
        for i in candidates:
            addition = min(bound - given[i], max(1, budget * loads[i] // whole), surplus)
            given[i] = given[i] + addition
            surplus = surplus - addition
    return np.array([bound] + given)


def ragged_sizes(stream_key, count, total, limit, lean):
    if count == 2:
        one = jax.random.randint(stream_key, (), max(1, total - limit), min(limit, total - 1) + 1)
        return jnp.stack([one, total - one])
    tallies = jnp.asarray(split_up(count, total, limit, lean), jnp.int32)
    twos = (count - 1) // 2
    giver, receiver = tallies[1:1 + 2 * twos:2], tallies[2:2 + 2 * twos:2]
    room = jnp.minimum(giver - 1, limit - receiver)
    passed = jax.random.randint(jax.random.fold_in(stream_key, 1), (twos,), 0, 1 << 20) % (room + 1)
    tallies = tallies.at[1:1 + 2 * twos:2].set(giver - passed).at[2:2 + 2 * twos:2].set(receiver + passed)
    return tallies[jax.random.permutation(jax.random.fold_in(stream_key, 2), count)]


def scatter_about(stream_key, dims, scale, most, cuts=(), kind=jnp.bfloat16):
    loudness = shard_levels(stream_key, dims, cuts, -0.22, 0.18) if cuts else 1.0
    array = jax.random.normal(stream_key, dims, jnp.float32) * scale * loudness
    return jnp.minimum(jnp.maximum(array, -most), most).astype(kind)


def setup_inputs(seed: int = 0) -> dict:
    key_list = jax.random.split(jax.random.key(seed), 13)
    saved = draw_saved(jax.random.fold_in(key_list[12], 71), 0)
    incoming = scatter_about(key_list[1], (SECTIONS, ROWS, D), 1.0, 6.0, ((0, 32), (2, 16)))
    gain = jnp.clip(1.0 + 0.1 * jax.random.normal(key_list[2], (SECTIONS, D), jnp.float32), 0.5, 1.5).astype(jnp.bfloat16)
    w_query = scatter_about(key_list[3], (SECTIONS, D, HEADS * HD), D ** -0.5, 0.09375, ((0, 32), (2, 16)))
    w_key = scatter_about(key_list[4], (SECTIONS, D, KV * HD), D ** -0.5, 0.09375, ((0, 32), (2, 16)))
    w_value = scatter_about(key_list[5], (SECTIONS, D, KV * HD), D ** -0.5, 0.09375, ((0, 32), (2, 16)))
    w_out = scatter_about(key_list[6], (SECTIONS, HEADS * HD, D), (HEADS * HD) ** -0.5, 0.09375, ((0, 32), (1, 16)))
    seg_lengths = jax.vmap(lambda own: ragged_sizes(own, SEGS, ROWS, MOST_SEG, 2))(jax.random.split(key_list[7], SECTIONS * TICKS)).reshape((SECTIONS, TICKS, SEGS)).astype(jnp.int32)
    score_grad = scatter_about(key_list[8], (TICKS, ROWS, D), 1.0, 6.0, ((2, 16),))
    rewards = scatter_about(key_list[9], (SAMPLES,), 1.0, 3.0, (), jnp.float32)
    sample_group = draw_sample_group(jax.random.fold_in(key_list[12], 71), 0)
    head_sample = plant(jax.random.randint(key_list[11], (TICKS, ROWS), 0, SAMPLES), jax.random.fold_in(key_list[11], 1), 0, SAMPLES - 1).astype(jnp.int32)
    return dict(saved=saved, incoming=incoming, gain=gain, w_query=w_query, w_key=w_key, w_value=w_value, w_out=w_out, seg_lengths=seg_lengths, score_grad=score_grad, rewards=rewards, sample_group=sample_group, head_sample=head_sample)


EPS = 1e-05
THETA = 500000.0

def rotate_pairs(values, positions, offset, direction):
    total_width = values.shape[1]
    column = (offset + jnp.arange(total_width, dtype=jnp.int32)) % HD
    pair_index = (column // 2).astype(jnp.float32)
    frequency = jnp.exp(pair_index * (-2.0 * math.log(THETA) / HD))
    angles = positions.astype(jnp.float32)[:, None] * frequency[None, :]
    parity = jnp.where(column % 2 == 0, -1.0, 1.0).astype(jnp.float32) * direction
    partner = values.reshape(values.shape[0], total_width // 2, 2)[:, :, ::-1].reshape(values.shape[0], total_width)
    return values * jnp.cos(angles) + partner * parity * jnp.sin(angles)

def row_layout(lengths):
    row_ids = jnp.arange(ROWS, dtype=jnp.int32)
    seg_ends = jnp.cumsum(lengths).astype(jnp.int32)
    segment = lax.optimization_barrier(jnp.sum((row_ids[:, None] >= seg_ends[None, :]).astype(jnp.int32), axis=1))
    member = segment[:, None] == jnp.arange(lengths.shape[0], dtype=jnp.int32)[None, :]
    begins = lax.optimization_barrier(jnp.sum(jnp.where(member, (seg_ends - lengths)[None, :], 0), axis=1))
    positions = row_ids - begins
    allowed = (segment[:, None] == segment[None, :]) & (row_ids[None, :] <= row_ids[:, None])
    return (positions, allowed)

def advantages(rewards, sample_group):
    member = (sample_group[:, None] == jnp.arange(GROUPS, dtype=jnp.int32)[None, :]).astype(jnp.float32)
    totals = lax.optimization_barrier(jnp.sum(member * rewards[:, None], axis=0))
    own_total = lax.optimization_barrier(jnp.sum(member * totals[None, :], axis=1))
    return rewards - (own_total - rewards) / (GROUP_SIZE - 1)

def head_gradient(advantage, head_sample, score_grad):
    chosen = head_sample[:, :, None] == jnp.arange(advantage.shape[0], dtype=jnp.int32)[None, None, :]
    row_adv = lax.optimization_barrier(jnp.sum(jnp.where(chosen, advantage[None, None, :], 0.0), axis=2))
    return (-row_adv[:, :, None] * score_grad.astype(jnp.float32)).astype(jnp.bfloat16)

def attention_grads(query_heads, key_heads, value_heads, dout_heads, allowed):
    score_scale = 1.0 / math.sqrt(HD)
    query32 = query_heads.astype(jnp.float32)
    keys32 = key_heads.astype(jnp.float32)
    values32 = value_heads.astype(jnp.float32)
    dout32 = dout_heads.astype(jnp.float32)
    scores = jnp.einsum('hrd,hcd->hrc', query32, keys32) * score_scale
    weights = jnp.where(allowed[None, :, :], jnp.exp(scores), 0.0)
    softmax = weights / lax.optimization_barrier(jnp.sum(weights, axis=2, keepdims=True))
    softmax_low = lax.optimization_barrier(softmax.astype(jnp.bfloat16)).astype(jnp.float32)
    dprobs = jnp.einsum('hrd,hcd->hrc', dout32, values32)
    dvalues = jnp.einsum('hrc,hrd->hcd', softmax_low, dout32)
    row_delta = lax.optimization_barrier(jnp.sum(softmax * dprobs, axis=2, keepdims=True))
    dscores = lax.optimization_barrier((softmax * (dprobs - row_delta) * score_scale).astype(jnp.bfloat16)).astype(jnp.float32)
    dquery = jnp.einsum('hrc,hcd->hrd', dscores, keys32)
    dkey_rows = jnp.einsum('hrc,hrd->hcd', dscores, query32)
    return (dquery, dkey_rows, dvalues)

def section_backward(saved_rows, grad_rows, gain, w_query, w_key, w_value, w_out, lengths):
    rows32 = saved_rows.astype(jnp.float32)
    inverse = lax.rsqrt(lax.optimization_barrier(jnp.mean(rows32 * rows32, axis=1, keepdims=True)) + EPS)
    gain32 = gain.astype(jnp.float32)[None, :]
    normed = (rows32 * inverse * gain32).astype(jnp.bfloat16)
    positions, allowed = row_layout(lengths)
    query_rows = rotate_pairs(jnp.dot(normed, w_query, preferred_element_type=jnp.float32), positions, 0, 1.0).astype(jnp.bfloat16)
    key_rows = rotate_pairs(jnp.dot(normed, w_key, preferred_element_type=jnp.float32), positions, 0, 1.0).astype(jnp.bfloat16)
    value_rows = jnp.dot(normed, w_value, preferred_element_type=jnp.float32).astype(jnp.bfloat16)
    dout_rows = jnp.dot(grad_rows, w_out.T, preferred_element_type=jnp.float32).astype(jnp.bfloat16)
    per_group = HEADS // KV
    query_heads = query_rows.reshape(ROWS, HEADS, HD).transpose(1, 0, 2)
    key_heads = jnp.repeat(key_rows.reshape(ROWS, KV, HD).transpose(1, 0, 2), per_group, axis=0)
    value_heads = jnp.repeat(value_rows.reshape(ROWS, KV, HD).transpose(1, 0, 2), per_group, axis=0)
    dout_heads = dout_rows.reshape(ROWS, HEADS, HD).transpose(1, 0, 2)
    dquery, dkey_rows, dvalues = attention_grads(query_heads, key_heads, value_heads, dout_heads, allowed)
    dquery = rotate_pairs(dquery.transpose(1, 0, 2).reshape(ROWS, HEADS * HD), positions, 0, -1.0).astype(jnp.bfloat16)
    dkey_rows = dkey_rows.reshape(KV, per_group, ROWS, HD).sum(axis=1).transpose(1, 0, 2).reshape(ROWS, KV * HD)
    dkey_rows = rotate_pairs(dkey_rows, positions, 0, -1.0).astype(jnp.bfloat16)
    dvalues = dvalues.reshape(KV, per_group, ROWS, HD).sum(axis=1).transpose(1, 0, 2).reshape(ROWS, KV * HD).astype(jnp.bfloat16)
    query_share = HEADS * HD // N_TP
    kv_share = KV * HD // N_TP
    partial_value = jnp.einsum('rtc,dtc->trd', dquery.reshape(ROWS, N_TP, query_share).astype(jnp.float32), w_query.reshape(D, N_TP, query_share).astype(jnp.float32))
    partial_value = partial_value + jnp.einsum('rtc,dtc->trd', dkey_rows.reshape(ROWS, N_TP, kv_share).astype(jnp.float32), w_key.reshape(D, N_TP, kv_share).astype(jnp.float32))
    partial_value = partial_value + jnp.einsum('rtc,dtc->trd', dvalues.reshape(ROWS, N_TP, kv_share).astype(jnp.float32), w_value.reshape(D, N_TP, kv_share).astype(jnp.float32))
    dnormed = lax.optimization_barrier(jnp.sum(lax.optimization_barrier(partial_value.astype(jnp.bfloat16)).astype(jnp.float32), axis=0))
    moment = lax.optimization_barrier(jnp.sum(rows32 * gain32 * dnormed, axis=1, keepdims=True)) / D
    result = grad_rows.astype(jnp.float32) + inverse * gain32 * dnormed - rows32 * inverse ** 3 * moment
    return result.astype(jnp.bfloat16)

def reference(saved, incoming, gain, w_query, w_key, w_value, w_out, seg_lengths, score_grad, rewards, sample_group, head_sample):
    head_rows = head_gradient(advantages(rewards, sample_group), head_sample, score_grad)
    grad_state = incoming
    emitted = []
    for tick_index in range(TICKS):
        section_out = lax.map(lambda packed: section_backward(*packed), (saved[:, tick_index], grad_state, gain, w_query, w_key, w_value, w_out, seg_lengths[:, tick_index]))
        emitted.append(section_out)
        grad_state = jnp.concatenate([section_out[1:], head_rows[tick_index][None]], axis=0)
    return (jnp.stack(emitted, axis=1), grad_state)
```

```python
import math

import jax
import jax.numpy as jnp
from jax import lax
from jax.experimental import pallas as pl
from jax.experimental.pallas import tpu as pltpu
from jax.sharding import PartitionSpec as P

D = 4096
KV = 4
HD = 128
ROWS = 128
TICKS = 2
GROUP_SIZE = 16
GROUPS = 32

EPS = 1e-05
THETA = 500000.0
SCALE = 1.0 / math.sqrt(HD)
F32 = jnp.float32
BF16 = jnp.bfloat16
VMEM_LIMIT = 48 * 1024 * 1024


def nn(a, b):
    return lax.dot_general(a, b, (((1,), (0,)), ((), ())), preferred_element_type=F32)


def nt(a, b):
    return lax.dot_general(a, b, (((1,), (1,)), ((), ())), preferred_element_type=F32)


def tn(a, b):
    return lax.dot_general(a, b, (((0,), (0,)), ((), ())), preferred_element_type=F32)


def pair_swap(v, axis):
    n = v.shape[axis]
    even = lax.broadcasted_iota(jnp.int32, v.shape, axis) % 2 == 0
    return jnp.where(even, pltpu.roll(v, n - 1, axis), pltpu.roll(v, 1, axis))


def kernel_call(body, outs, *args):
    vmem = pl.BlockSpec(memory_space=pltpu.VMEM)
    return pl.pallas_call(
        body,
        out_shape=outs,
        in_specs=[vmem] * len(args),
        out_specs=[vmem] * len(outs),
        compiler_params=pltpu.CompilerParams(vmem_limit_bytes=VMEM_LIMIT),
    )(*args)


def forward_body(
    x_ref, gain_ref, wq_ref, wkv_ref, cos_ref, sin_ref, cost_ref, sint_ref, q_ref, kv_ref, inv_ref
):
    blocks, rows, width = x_ref.shape
    squares = jnp.zeros((rows, width), F32)
    for j in range(blocks):
        xj = x_ref[j].astype(F32)
        squares = squares + xj * xj
    inverse = lax.rsqrt(jnp.sum(squares, axis=1, keepdims=True) * (1.0 / D) + EPS)
    inv_ref[...] = inverse
    query = jnp.zeros(q_ref.shape, F32)
    kvt = jnp.zeros(kv_ref.shape[1:], F32)
    for j in range(blocks):
        part = slice(j * width, (j + 1) * width)
        normed = (x_ref[j].astype(F32) * inverse * gain_ref[:, part].astype(F32)).astype(BF16)
        query = query + nn(normed, wq_ref[part, :])
        kvt = kvt + nt(wkv_ref[:, part], normed)
    for h in range(query.shape[1] // HD):
        cols = slice(h * HD, (h + 1) * HD)
        head = query[:, cols]
        q_ref[:, cols] = (head * cos_ref[...] + pair_swap(head, 1) * sin_ref[...]).astype(BF16)
    half = kvt.shape[0] // 2
    keys = kvt[:half]
    keys = keys * cost_ref[...] + pair_swap(keys, 0) * sint_ref[...]
    both = jnp.concatenate([keys, kvt[half:]], axis=0).astype(BF16)
    for i in range(kv_ref.shape[0]):
        kv_ref[i] = both


def attention_body(
    dy_ref, wo_ref, q_ref, kv_ref, mask_ref, cos_ref, sin_ref, dq_ref, dkv_ref, t_ref
):
    blocks, rows, width = dy_ref.shape
    dout = jnp.zeros(dq_ref.shape, F32)
    for j in range(blocks):
        dout = dout + nt(dy_ref[j], wo_ref[:, j * width : (j + 1) * width])
    dout = dout.astype(BF16)
    shares, both, _ = kv_ref.shape
    half = both // 2
    keys = jnp.concatenate([kv_ref[i, :half] for i in range(shares)], axis=0)
    values = jnp.concatenate([kv_ref[i, half:] for i in range(shares)], axis=0)
    allowed = mask_ref[...] > 0.0
    dkeys = jnp.zeros((HD, rows), F32)
    dvalues = jnp.zeros((HD, rows), F32)
    own = jnp.zeros((rows, HD), F32)
    for h in range(dq_ref.shape[1] // HD):
        cols = slice(h * HD, (h + 1) * HD)
        query = q_ref[:, cols]
        dhead = dout[:, cols]
        weights = jnp.where(allowed, jnp.exp(nn(query, keys) * SCALE), 0.0)
        softmax = weights / jnp.sum(weights, axis=1, keepdims=True)
        dprobs = nn(dhead, values)
        delta = jnp.sum(softmax * dprobs, axis=1, keepdims=True)
        dscores = (softmax * (dprobs - delta) * SCALE).astype(BF16)
        dquery = nt(dscores, keys)
        dkeys = dkeys + tn(query, dscores)
        dvalues = dvalues + tn(dhead, softmax.astype(BF16))
        own = own + dquery * query.astype(F32)
        dq_ref[:, cols] = (dquery * cos_ref[...] - pair_swap(dquery, 1) * sin_ref[...]).astype(BF16)
    shared = dkeys * keys.astype(F32) + dvalues * values.astype(F32)
    t_ref[...] = jnp.sum(own + shared.T, axis=1, keepdims=True)
    for i in range(shares):
        part = slice(i * half, (i + 1) * half)
        dkv_ref[i, :half] = dkeys[part].astype(BF16)
        dkv_ref[i, half:] = dvalues[part].astype(BF16)


def partial_body(
    dq_ref, dkv_ref, wq_ref, wkv_ref, x_ref, gain_ref, inv_ref, t_ref, cost_ref, sint_ref, out_ref
):
    blocks, _, width = x_ref.shape
    dkv = dkv_ref[0].astype(F32)
    for i in range(1, dkv_ref.shape[0]):
        dkv = dkv + dkv_ref[i].astype(F32)
    half = dkv.shape[0] // 2
    dkeys = dkv[:half]
    dkeys = dkeys * cost_ref[...] - pair_swap(dkeys, 0) * sint_ref[...]
    dkv = jnp.concatenate([dkeys, dkv[half:]], axis=0).astype(BF16)
    dq = dq_ref[...]
    inverse = inv_ref[...]
    along = inverse * inverse * t_ref[...] * (1.0 / D)
    for j in range(blocks):
        part = slice(j * width, (j + 1) * width)
        total = nt(dq, wq_ref[part, :]) + tn(dkv, wkv_ref[:, part])
        scaled = total * (inverse * gain_ref[:, part].astype(F32))
        out_ref[j] = (scaled - x_ref[j].astype(F32) * along).astype(BF16)


def shifted(value, axis, steps):
    count = lax.axis_size(axis)
    first, last = (max(0, -steps), min(count, count - steps))
    return lax.ppermute(value, axis, [(source, source + steps) for source in range(first, last)])


def rotation_tables(positions):
    column = jnp.arange(HD, dtype=jnp.int32)
    pair_index = (column // 2).astype(F32)
    frequency = jnp.exp(pair_index * (-2.0 * math.log(THETA) / HD))
    angles = positions.astype(F32)[:, None] * frequency[None, :]
    parity = jnp.where(column % 2 == 0, -1.0, 1.0).astype(F32)
    return jnp.cos(angles), jnp.sin(angles) * parity


def row_layout(lengths):
    row_ids = jnp.arange(ROWS, dtype=jnp.int32)
    seg_ends = jnp.cumsum(lengths)
    segment = jnp.sum((row_ids[:, None] >= seg_ends[None, :]).astype(jnp.int32), axis=1)
    member = segment[:, None] == jnp.arange(lengths.shape[0], dtype=jnp.int32)[None, :]
    begins = jnp.sum(jnp.where(member, (seg_ends - lengths)[None, :], 0), axis=1)
    positions = row_ids - begins
    allowed = (segment[:, None] == segment[None, :]) & (row_ids[None, :] <= row_ids[:, None])
    return (positions, allowed)


def advantages(rewards, sample_group):
    member = (sample_group[:, None] == jnp.arange(GROUPS, dtype=jnp.int32)[None, :]).astype(F32)
    totals = jnp.sum(member * rewards[:, None], axis=0)
    own_total = jnp.sum(member * totals[None, :], axis=1)
    return rewards - (own_total - rewards) / (GROUP_SIZE - 1)


def head_gradient(advantage, head_sample, score_grad):
    chosen = (
        head_sample[:, :, None] == jnp.arange(advantage.shape[0], dtype=jnp.int32)[None, None, :]
    )
    row_adv = jnp.sum(jnp.where(chosen, advantage[None, None, :], 0.0), axis=2)
    return (-row_adv[:, :, None] * score_grad.astype(F32)).astype(BF16)


def per_device(
    saved,
    incoming,
    gain,
    w_query,
    w_key,
    w_value,
    w_out,
    seg_lengths,
    score_grad,
    rewards,
    sample_group,
    head_sample,
):
    tp_index = lax.axis_index("tp")
    tp_count = lax.axis_size("tp")
    last_section = lax.axis_index("pipe") == lax.axis_size("pipe") - 1
    share = tp_count // KV
    groups = [list(range(g * share, (g + 1) * share)) for g in range(KV)]
    kv_share = w_key.shape[2]
    kv_start = (tp_index % share) * kv_share
    wq = w_query[0]
    wkv = jnp.concatenate([w_key[0].T, w_value[0].T], axis=0)
    wo = w_out[0]

    def to_all(block):
        return lax.all_to_all(
            jnp.broadcast_to(block[None], (tp_count,) + block.shape), "tp", 0, 0
        )

    def in_group(blocks):
        return lax.all_to_all(blocks, "tp", 0, 0, axis_index_groups=groups)

    x_next = lax.all_gather(saved[0, 1], "tp", axis=0)
    x_full = to_all(saved[0, 0])
    grad, x_full = lax.optimization_barrier((incoming[0], x_full))
    grad_full = to_all(grad)
    head_rows = head_gradient(advantages(rewards, sample_group), head_sample, score_grad)

    def forward(tick, rows_full):
        positions, allowed = row_layout(seg_lengths[0, tick])
        cos, sin = rotation_tables(positions)
        cos_t = lax.dynamic_slice_in_dim(cos.T, kv_start, kv_share, 0)
        sin_t = lax.dynamic_slice_in_dim(sin.T, kv_start, kv_share, 0)
        query, kv, inverse = kernel_call(
            forward_body,
            (
                jax.ShapeDtypeStruct((ROWS, wq.shape[1]), BF16),
                jax.ShapeDtypeStruct((share, 2 * kv_share, ROWS), BF16),
                jax.ShapeDtypeStruct((ROWS, 1), F32),
            ),
            rows_full, gain, wq, wkv, cos, sin, cos_t, sin_t,
        )
        return query, in_group(kv), inverse, allowed.astype(F32), cos, sin, cos_t, sin_t

    outputs = []
    for tick in range(TICKS):
        rows_full = x_full if tick == 0 else x_next
        query, kv, inverse, mask, cos, sin, cos_t, sin_t = forward(tick, rows_full)
        dquery, dkv, along = kernel_call(
            attention_body,
            (
                jax.ShapeDtypeStruct(query.shape, BF16),
                jax.ShapeDtypeStruct(kv.shape, BF16),
                jax.ShapeDtypeStruct((ROWS, 1), F32),
            ),
            grad_full, wo, query, kv, mask, cos, sin,
        )
        dkv = in_group(dkv)
        (blocks,) = kernel_call(
            partial_body,
            (jax.ShapeDtypeStruct(rows_full.shape, BF16),),
            dquery, dkv, wq, wkv, rows_full, gain, inverse, along, cos_t, sin_t,
        )
        blocks = lax.all_to_all(blocks, "tp", 0, 0)
        result = (grad.astype(F32) + jnp.sum(blocks.astype(F32), axis=0)).astype(BF16)
        outputs.append(result)
        grad = jnp.where(last_section, head_rows[tick], shifted(result, "pipe", -1))
        if tick + 1 < TICKS:
            grad_full = to_all(grad)
    return (jnp.stack(outputs, axis=0)[None], grad[None])


def solution(mesh):
    placed = (
        P("pipe", None, None, "tp"),
        P("pipe", None, "tp"),
        P("pipe", None),
        P("pipe", None, "tp"),
        P("pipe", None, "tp"),
        P("pipe", None, "tp"),
        P("pipe", "tp", None),
        P("pipe", None, None),
        P(None, None, "tp"),
        P(),
        P(),
        P(),
    )
    return jax.shard_map(
        per_device,
        mesh=mesh,
        in_specs=placed,
        out_specs=(P("pipe", None, None, "tp"), P("pipe", None, "tp")),
        check_vma=False,
    )
```

```python
import math

import jax
import jax.numpy as jnp
from jax import lax
from jax.experimental import pallas as pl
from jax.experimental.pallas import tpu as pltpu
from jax.sharding import PartitionSpec as P

D = 4096
KV = 4
HD = 128
ROWS = 128
TICKS = 2
GROUP_SIZE = 16
GROUPS = 32

EPS = 1e-05
THETA = 500000.0
SCALE = 1.0 / math.sqrt(HD)
F32 = jnp.float32
BF16 = jnp.bfloat16
VMEM_LIMIT = 12 * 1024 * 1024


def nn(a, b):
    return lax.dot_general(a, b, (((1,), (0,)), ((), ())), preferred_element_type=F32)


def nt(a, b):
    return lax.dot_general(a, b, (((1,), (1,)), ((), ())), preferred_element_type=F32)


def tn(a, b):
    return lax.dot_general(a, b, (((0,), (0,)), ((), ())), preferred_element_type=F32)


def pair_swap(v, axis):
    n = v.shape[axis]
    even = lax.broadcasted_iota(jnp.int32, v.shape, axis) % 2 == 0
    return jnp.where(even, pltpu.roll(v, n - 1, axis), pltpu.roll(v, 1, axis))


def kernel_call(body, outs, specs, args):
    vmem = pl.BlockSpec(memory_space=pltpu.VMEM)
    kinds = {
        "v": vmem,
        "s": pl.BlockSpec(memory_space=pltpu.SMEM),
    }
    return pl.pallas_call(
        body,
        out_shape=outs,
        in_specs=[kinds[kind] for kind in specs],
        out_specs=[vmem] * len(outs),
        compiler_params=pltpu.CompilerParams(vmem_limit_bytes=VMEM_LIMIT),
    )(*args)


def forward_body(
    x_ref,
    wq_ref,
    wk_ref,
    wv_ref,
    gain_ref,
    cos_ref,
    sin_ref,
    cost_ref,
    sint_ref,
    q_ref,
    kv_ref,
    inv_ref,
):
    blocks, rows, width = x_ref.shape
    squares = jnp.zeros((rows, width), F32)
    for j in range(blocks):
        xj = x_ref[j].astype(F32)
        squares = squares + xj * xj
    inverse = lax.rsqrt(jnp.sum(squares, axis=1, keepdims=True) * (1.0 / D) + EPS)
    inv_ref[...] = inverse
    query = jnp.zeros(q_ref.shape, F32)
    half = wk_ref.shape[0]
    keys = jnp.zeros((half, rows), F32)
    values = jnp.zeros((half, rows), F32)
    for j in range(blocks):
        part = slice(j * width, (j + 1) * width)
        normed = (x_ref[j].astype(F32) * inverse * gain_ref[:, part].astype(F32)).astype(BF16)
        query = query + nn(normed, wq_ref[part, :])
        keys = keys + nt(wk_ref[:, part], normed)
        values = values + nt(wv_ref[:, part], normed)
    for h in range(query.shape[1] // HD):
        cols = slice(h * HD, (h + 1) * HD)
        head = query[:, cols]
        q_ref[:, cols] = (head * cos_ref[...] + pair_swap(head, 1) * sin_ref[...]).astype(BF16)
    keys = keys * cost_ref[...] + pair_swap(keys, 0) * sint_ref[...]
    kv_ref[...] = jnp.concatenate([keys, values], axis=1).astype(BF16)


def pack_body(grad_ref, kv_ref, out_ref):
    rows = grad_ref.shape[0]
    for i in range(out_ref.shape[0]):
        out_ref[i, :rows] = grad_ref[...]
        out_ref[i, rows:] = kv_ref[...]


def attention_body(
    place_ref,
    got_ref,
    wo_ref,
    q_ref,
    mask_ref,
    cos_ref,
    sin_ref,
    dq_ref,
    dkv_ref,
    t_ref,
):
    blocks, _, width = got_ref.shape
    rows = q_ref.shape[0]
    shares, half = dkv_ref.shape[0], dkv_ref.shape[1] // 2
    kv = [got_ref[place_ref[0] + i, rows:] for i in range(shares)]
    keys = jnp.concatenate([part[:, :rows] for part in kv], axis=0)
    values = jnp.concatenate([part[:, rows:] for part in kv], axis=0)
    allowed = mask_ref[...] > 0.0
    soft = []
    for h in range(dq_ref.shape[1] // HD):
        query = q_ref[:, h * HD : (h + 1) * HD]
        weights = jnp.where(allowed, jnp.exp(nn(query, keys) * SCALE), 0.0)
        soft.append(weights / jnp.sum(weights, axis=1, keepdims=True))
    dout = jnp.zeros(dq_ref.shape, F32)
    for j in range(blocks):
        dout = dout + nt(got_ref[j, :rows], wo_ref[:, j * width : (j + 1) * width])
    dout = dout.astype(BF16)
    dkeys = jnp.zeros((HD, rows), F32)
    dvalues = jnp.zeros((HD, rows), F32)
    own = jnp.zeros((rows, HD), F32)
    for h in range(dq_ref.shape[1] // HD):
        cols = slice(h * HD, (h + 1) * HD)
        query = q_ref[:, cols]
        dhead = dout[:, cols]
        softmax = soft[h]
        dprobs = nn(dhead, values)
        delta = jnp.sum(softmax * dprobs, axis=1, keepdims=True)
        dscores = (softmax * (dprobs - delta) * SCALE).astype(BF16)
        dquery = nt(dscores, keys)
        dkeys = dkeys + tn(query, dscores)
        dvalues = dvalues + tn(dhead, softmax.astype(BF16))
        own = own + dquery * query.astype(F32)
        dq_ref[:, cols] = (dquery * cos_ref[...] - pair_swap(dquery, 1) * sin_ref[...]).astype(BF16)
    shared = dkeys * keys.astype(F32) + dvalues * values.astype(F32)
    t_ref[...] = jnp.sum(own + shared.T, axis=1, keepdims=True)
    for i in range(shares):
        part = slice(i * half, (i + 1) * half)
        dkv_ref[i, :half] = dkeys[part].astype(BF16)
        dkv_ref[i, half:] = dvalues[part].astype(BF16)


def partial_body(
    x_ref,
    dq_ref,
    dkv_ref,
    wq_ref,
    wk_ref,
    wv_ref,
    gain_ref,
    inv_ref,
    t_ref,
    cost_ref,
    sint_ref,
    out_ref,
):
    blocks, _, width = x_ref.shape
    dkv = dkv_ref[0].astype(F32)
    for i in range(1, dkv_ref.shape[0]):
        dkv = dkv + dkv_ref[i].astype(F32)
    half = dkv.shape[0] // 2
    dkeys = dkv[:half]
    dkeys = (dkeys * cost_ref[...] - pair_swap(dkeys, 0) * sint_ref[...]).astype(BF16)
    dvalues = dkv[half:].astype(BF16)
    dq = dq_ref[...]
    inverse = inv_ref[...]
    along = inverse * inverse * t_ref[...] * (1.0 / D)
    for j in range(blocks):
        part = slice(j * width, (j + 1) * width)
        total = nt(dq, wq_ref[part, :])
        total = total + tn(dkeys, wk_ref[:, part]) + tn(dvalues, wv_ref[:, part])
        scaled = total * (inverse * gain_ref[:, part].astype(F32))
        out_ref[j] = (scaled - x_ref[j].astype(F32) * along).astype(BF16)


def shifted(value, axis, steps):
    count = lax.axis_size(axis)
    first, last = (max(0, -steps), min(count, count - steps))
    return lax.ppermute(value, axis, [(source, source + steps) for source in range(first, last)])


def rotation_tables(positions):
    column = jnp.arange(HD, dtype=jnp.int32)
    pair_index = (column // 2).astype(F32)
    frequency = jnp.exp(pair_index * (-2.0 * math.log(THETA) / HD))
    angles = positions.astype(F32)[:, None] * frequency[None, :]
    parity = jnp.where(column % 2 == 0, -1.0, 1.0).astype(F32)
    return jnp.cos(angles), jnp.sin(angles) * parity


def row_layout(lengths):
    row_ids = jnp.arange(ROWS, dtype=jnp.int32)
    seg_ends = jnp.cumsum(lengths)
    segment = jnp.sum((row_ids[:, None] >= seg_ends[None, :]).astype(jnp.int32), axis=1)
    member = segment[:, None] == jnp.arange(lengths.shape[0], dtype=jnp.int32)[None, :]
    begins = jnp.sum(jnp.where(member, (seg_ends - lengths)[None, :], 0), axis=1)
    positions = row_ids - begins
    allowed = (segment[:, None] == segment[None, :]) & (row_ids[None, :] <= row_ids[:, None])
    return (positions, allowed)


def advantages(rewards, sample_group):
    member = (sample_group[:, None] == jnp.arange(GROUPS, dtype=jnp.int32)[None, :]).astype(F32)
    totals = jnp.sum(member * rewards[:, None], axis=0)
    own_total = jnp.sum(member * totals[None, :], axis=1)
    return rewards - (own_total - rewards) / (GROUP_SIZE - 1)


def head_gradient(advantage, head_sample, score_grad):
    chosen = (
        head_sample[:, :, None] == jnp.arange(advantage.shape[0], dtype=jnp.int32)[None, None, :]
    )
    row_adv = jnp.sum(jnp.where(chosen, advantage[None, None, :], 0.0), axis=2)
    return (-row_adv[:, :, None] * score_grad.astype(F32)).astype(BF16)


def per_device(
    saved,
    incoming,
    gain,
    w_query,
    w_key,
    w_value,
    w_out,
    seg_lengths,
    score_grad,
    rewards,
    sample_group,
    head_sample,
):
    tp_index = lax.axis_index("tp")
    tp_count = lax.axis_size("tp")
    last_section = lax.axis_index("pipe") == lax.axis_size("pipe") - 1
    share = tp_count // KV
    groups = [list(range(g * share, (g + 1) * share)) for g in range(KV)]
    wq, wk, wv, wo = w_query[0], w_key[0].T, w_value[0].T, w_out[0]
    kv_share = wk.shape[0]
    base = (tp_index // share * share).astype(jnp.int32)[None]
    kv_start = tp_index % share * kv_share
    full_shape = (tp_count, ROWS, saved.shape[3])

    def tables_of(tick):
        positions, allowed = row_layout(seg_lengths[0, tick])
        cos, sin = rotation_tables(positions)
        cos_t = lax.dynamic_slice_in_dim(cos.T, kv_start, kv_share, 0)
        sin_t = lax.dynamic_slice_in_dim(sin.T, kv_start, kv_share, 0)
        return allowed.astype(F32), cos, sin, cos_t, sin_t

    def forward(rows_full, cos, sin, cos_t, sin_t):
        return kernel_call(
            forward_body,
            (
                jax.ShapeDtypeStruct((ROWS, wq.shape[1]), BF16),
                jax.ShapeDtypeStruct((kv_share, 2 * ROWS), BF16),
                jax.ShapeDtypeStruct((ROWS, 1), F32),
            ),
            "v" * 9,
            (rows_full, wq, wk, wv, gain, cos, sin, cos_t, sin_t),
        )

    x_all = lax.all_gather(saved[0], "tp", axis=1)
    x_first = lax.all_to_all(
        jnp.broadcast_to(saved[0, 0][None], full_shape), "tp", 0, 0
    )
    head_rows = head_gradient(advantages(rewards, sample_group), head_sample, score_grad)
    tables = [tables_of(tick) for tick in range(TICKS)]
    x_first, head_rows, tables, base, last_section = lax.optimization_barrier(
        (x_first, head_rows, tables, base, last_section)
    )
    grad = incoming[0]

    outputs = []
    for tick in range(TICKS):
        rows_full = x_first if tick == 0 else x_all[tick]
        mask, cos, sin, cos_t, sin_t = tables[tick]
        query, kv, inverse = forward(rows_full, cos, sin, cos_t, sin_t)
        (packed,) = kernel_call(
            pack_body,
            (jax.ShapeDtypeStruct((tp_count, ROWS + kv_share, grad.shape[1]), BF16),),
            "vv",
            (grad, kv),
        )
        got = lax.all_to_all(packed, "tp", 0, 0)
        dquery, dkv, along = kernel_call(
            attention_body,
            (
                jax.ShapeDtypeStruct(query.shape, BF16),
                jax.ShapeDtypeStruct((share, 2 * kv_share, ROWS), BF16),
                jax.ShapeDtypeStruct((ROWS, 1), F32),
            ),
            "s" + "v" * 6,
            (base, got, wo, query, mask, cos, sin),
        )
        dkv = lax.all_to_all(dkv, "tp", 0, 0, axis_index_groups=groups)
        (blocks,) = kernel_call(
            partial_body,
            (jax.ShapeDtypeStruct(full_shape, BF16),),
            "v" * 11,
            (rows_full, dquery, dkv, wq, wk, wv, gain, inverse, along, cos_t, sin_t),
        )
        blocks = lax.all_to_all(blocks, "tp", 0, 0)
        result = (grad.astype(F32) + jnp.sum(blocks.astype(F32), axis=0)).astype(BF16)
        grad = jnp.where(last_section, head_rows[tick], shifted(result, "pipe", -1))
        result, grad = lax.optimization_barrier((result, grad))
        outputs.append(result)
    return (jnp.stack(outputs, axis=0)[None], grad[None])


def solution(mesh):
    placed = (
        P("pipe", None, None, "tp"),
        P("pipe", None, "tp"),
        P("pipe", None),
        P("pipe", None, "tp"),
        P("pipe", None, "tp"),
        P("pipe", None, "tp"),
        P("pipe", "tp", None),
        P("pipe", None, None),
        P(None, None, "tp"),
        P(),
        P(),
        P(),
    )
    return jax.shard_map(
        per_device,
        mesh=mesh,
        in_specs=placed,
        out_specs=(P("pipe", None, None, "tp"), P("pipe", None, "tp")),
        check_vma=False,
    )
```

```python
import functools
import math

import jax
import jax.numpy as jnp
import ml_dtypes
import numpy as np
from jax import lax
from jax.experimental import pallas as pl
from jax.experimental.pallas import tpu as pltpu
from jax.sharding import PartitionSpec as P

D = 4096
KV = 4
HD = 128
ROWS = 128
TICKS = 2
GROUP_SIZE = 16
GROUPS = 32

EPS = 1e-05
THETA = 500000.0
SCALE = 1.0 / math.sqrt(HD)
F32 = jnp.float32
BF16 = jnp.bfloat16
VMEM_LIMIT = 16 * 1024 * 1024
FIRST_ROWS = 64
MORE_ROWS = 32


def nn(a, b):
    return lax.dot_general(a, b, (((1,), (0,)), ((), ())), preferred_element_type=F32)


def nt(a, b):
    return lax.dot_general(a, b, (((1,), (1,)), ((), ())), preferred_element_type=F32)


def tn(a, b):
    return lax.dot_general(a, b, (((0,), (0,)), ((), ())), preferred_element_type=F32)


def pair_swap(v, axis):
    n = v.shape[axis]
    even = lax.broadcasted_iota(jnp.int32, v.shape, axis) % 2 == 0
    return jnp.where(even, pltpu.roll(v, n - 1, axis), pltpu.roll(v, 1, axis))


def kernel_call(body, outs, specs, args):
    vmem = pl.BlockSpec(memory_space=pltpu.VMEM)
    kinds = {
        "v": vmem,
        "s": pl.BlockSpec(memory_space=pltpu.SMEM),
    }
    return pl.pallas_call(
        body,
        out_shape=outs,
        in_specs=[kinds[kind] for kind in specs],
        out_specs=[vmem] * len(outs),
        compiler_params=pltpu.CompilerParams(vmem_limit_bytes=VMEM_LIMIT),
    )(*args)


def segment_starts(seg_ref, tick):
    lengths = seg_ref[0, tick : tick + 1, :].astype(F32)
    index = lax.broadcasted_iota(jnp.int32, lengths.shape, 1)
    return [
        jnp.sum(jnp.where(index < g, lengths, 0.0), axis=1, keepdims=True)
        for g in range(1, lengths.shape[1])
    ]


def iotas():
    row = lax.broadcasted_iota(jnp.int32, (ROWS, ROWS), 0).astype(F32)
    column = lax.broadcasted_iota(jnp.int32, (ROWS, ROWS), 1).astype(F32)
    return row, column


def position_match(seg_ref, tick):
    row, column = iotas()
    begin = jnp.zeros(row.shape, F32)
    for start in segment_starts(seg_ref, tick):
        begin = jnp.where(row >= start, start, begin)
    return jnp.where(column == row - begin, 1.0, 0.0).astype(BF16)


def spread_body(saved_ref, out_ref):
    rows = saved_ref.shape[2]
    for i in range(out_ref.shape[0]):
        out_ref[i, :rows] = saved_ref[0, 0]
        out_ref[i, rows:] = saved_ref[0, 1, : out_ref.shape[1] - rows]


def forward_body(
    tick,
    place_ref,
    seg_ref,
    wq_ref,
    wk_ref,
    wv_ref,
    gain_ref,
    ctab_ref,
    stab_ref,
    ctabt_ref,
    stabt_ref,
    *refs,
):
    if tick == 0:
        x_ref, q_ref, kv_ref, inv_ref, cos_ref, sin_ref, cost_ref, sint_ref = refs
    else:
        first, second, third, q_ref, kv_ref, inv_ref, cos_ref, sin_ref, cost_ref, sint_ref, x_ref = (
            refs
        )
        low = first.shape[1] - ROWS
        mid = low + second.shape[1] - ROWS - kv_ref.shape[0]
        for j in range(x_ref.shape[0]):
            x_ref[j, :low] = first[j, ROWS:]
            x_ref[j, low:mid] = second[j, ROWS + kv_ref.shape[0] :]
            x_ref[j, mid:] = third[j, ROWS:]
    blocks, _, width = x_ref.shape
    half = wk_ref.shape[0]
    match = position_match(seg_ref, tick)
    own = pl.ds(pl.multiple_of(place_ref[0] * half, half), half)
    cos = sum(nn(match, ctab_ref[i]) for i in range(3))
    sin = sum(nn(match, stab_ref[i]) for i in range(3))
    cos_t = sum(nt(ctabt_ref[i, own, :], match) for i in range(3))
    sin_t = sum(nt(stabt_ref[i, own, :], match) for i in range(3))
    cos_ref[...] = cos
    sin_ref[...] = sin
    cost_ref[...] = cos_t
    sint_ref[...] = sin_t
    squares = jnp.zeros((ROWS, width), F32)
    for j in range(blocks):
        xj = x_ref[j, :ROWS].astype(F32)
        squares = squares + xj * xj
    inverse = lax.rsqrt(jnp.sum(squares, axis=1, keepdims=True) * (1.0 / D) + EPS)
    inv_ref[...] = inverse
    query = jnp.zeros(q_ref.shape, F32)
    keys = jnp.zeros((half, ROWS), F32)
    values = jnp.zeros((half, ROWS), F32)
    for j in range(blocks):
        part = slice(j * width, (j + 1) * width)
        normed = x_ref[j, :ROWS].astype(F32) * inverse * gain_ref[:, part].astype(F32)
        normed = normed.astype(BF16)
        query = query + nn(normed, wq_ref[part, :])
        keys = keys + nt(wk_ref[:, part], normed)
        values = values + nt(wv_ref[:, part], normed)
    for h in range(query.shape[1] // HD):
        cols = slice(h * HD, (h + 1) * HD)
        head = query[:, cols]
        q_ref[:, cols] = (head * cos + pair_swap(head, 1) * sin).astype(BF16)
    keys = keys * cos_t + pair_swap(keys, 0) * sin_t
    kv_ref[...] = jnp.concatenate([keys, values], axis=1).astype(BF16)


def first_pack_body(early, grad_ref, kv_ref, saved_ref, out_ref):
    start = grad_ref.shape[0] + kv_ref.shape[0]
    for i in range(out_ref.shape[0]):
        out_ref[i, : grad_ref.shape[0]] = grad_ref[...]
        out_ref[i, grad_ref.shape[0] : start] = kv_ref[...]
        out_ref[i, start:] = saved_ref[0, 1, early : early + out_ref.shape[1] - start]


def pack_body(*refs):
    parts, out_ref = refs[:-1], refs[-1]
    for i in range(out_ref.shape[0]):
        start = 0
        for part in parts:
            out_ref[i, start : start + part.shape[0]] = part[...]
            start += part.shape[0]


def next_gradient(tick, last_ref, received_ref, score_ref, rewards_ref, group_ref, sample_ref, grad_ref):
    grad_ref[...] = received_ref[...]

    @pl.when(last_ref[0] > 0)
    def _():
        rewards = rewards_ref[...]
        samples = rewards.shape[1]
        prompt = lax.broadcasted_iota(jnp.int32, (GROUPS, samples), 0)
        member = prompt == group_ref[...]
        totals = jnp.sum(jnp.where(member, rewards, 0.0), axis=1, keepdims=True)
        own_total = jnp.sum(jnp.where(member, totals, 0.0), axis=0, keepdims=True)
        advantage = rewards - (own_total - rewards) / (GROUP_SIZE - 1)
        sample = lax.broadcasted_iota(jnp.int32, (ROWS, samples), 1)
        row, column = iotas()
        own = jnp.where(row == column, sample_ref[tick : tick + 1, :].astype(F32), 0.0)
        chosen = sample.astype(F32) == jnp.sum(own, axis=1, keepdims=True)
        row_adv = jnp.sum(jnp.where(chosen, advantage, 0.0), axis=1, keepdims=True)
        grad_ref[...] = (-row_adv * score_ref[tick].astype(F32)).astype(BF16)


def turn_body(
    tick,
    last_ref,
    received_ref,
    score_ref,
    rewards_ref,
    group_ref,
    sample_ref,
    kv_ref,
    grad_ref,
    out_ref,
):
    next_gradient(
        tick, last_ref, received_ref, score_ref, rewards_ref, group_ref, sample_ref, grad_ref
    )
    pack_body(grad_ref, kv_ref, out_ref)


def attention_body(
    tick,
    base_ref,
    seg_ref,
    got_ref,
    wo_ref,
    q_ref,
    cos_ref,
    sin_ref,
    dq_ref,
    dkv_ref,
    t_ref,
):
    blocks, _, width = got_ref.shape
    shares, half = dkv_ref.shape[0], dkv_ref.shape[1] // 2
    kv = [got_ref[base_ref[0] + i, ROWS : ROWS + half] for i in range(shares)]
    keys = jnp.concatenate([part[:, :ROWS] for part in kv], axis=0)
    values = jnp.concatenate([part[:, ROWS:] for part in kv], axis=0)
    row, column = iotas()
    allowed = column <= row
    for start in segment_starts(seg_ref, tick):
        allowed = allowed & ((row < start) | (column >= start))
    dout = jnp.zeros(dq_ref.shape, F32)
    for j in range(blocks):
        dout = dout + nt(got_ref[j, :ROWS], wo_ref[:, j * width : (j + 1) * width])
    dout = dout.astype(BF16)
    dkeys = jnp.zeros((HD, ROWS), F32)
    dvalues = jnp.zeros((HD, ROWS), F32)
    own = jnp.zeros((ROWS, HD), F32)
    for h in range(dq_ref.shape[1] // HD):
        cols = slice(h * HD, (h + 1) * HD)
        query = q_ref[:, cols]
        dhead = dout[:, cols]
        weights = jnp.where(allowed, jnp.exp(nn(query, keys) * SCALE), 0.0)
        softmax = weights / jnp.sum(weights, axis=1, keepdims=True)
        dprobs = nn(dhead, values)
        delta = jnp.sum(softmax * dprobs, axis=1, keepdims=True)
        dscores = (softmax * (dprobs - delta) * SCALE).astype(BF16)
        dquery = nt(dscores, keys)
        dkeys = dkeys + tn(query, dscores)
        dvalues = dvalues + tn(dhead, softmax.astype(BF16))
        own = own + dquery * query.astype(F32)
        dq_ref[:, cols] = (dquery * cos_ref[...] - pair_swap(dquery, 1) * sin_ref[...]).astype(BF16)
    shared = dkeys * keys.astype(F32) + dvalues * values.astype(F32)
    t_ref[...] = jnp.sum(own + shared.T, axis=1, keepdims=True)
    for i in range(shares):
        part = slice(i * half, (i + 1) * half)
        dkv_ref[i, :half] = dkeys[part].astype(BF16)
        dkv_ref[i, half:] = dvalues[part].astype(BF16)


def partial_body(
    middle,
    x_ref,
    dq_ref,
    dkv_ref,
    wq_ref,
    wk_ref,
    wv_ref,
    gain_ref,
    inv_ref,
    t_ref,
    cost_ref,
    sint_ref,
    *refs,
):
    out_ref = refs[-1]
    blocks, _, width = x_ref.shape
    dkv = dkv_ref[0].astype(F32)
    for i in range(1, dkv_ref.shape[0]):
        dkv = dkv + dkv_ref[i].astype(F32)
    half = dkv.shape[0] // 2
    dkeys = dkv[:half]
    dkeys = (dkeys * cost_ref[...] - pair_swap(dkeys, 0) * sint_ref[...]).astype(BF16)
    dvalues = dkv[half:].astype(BF16)
    dq = dq_ref[...]
    inverse = inv_ref[...]
    along = inverse * inverse * t_ref[...] * (1.0 / D)
    for j in range(blocks):
        part = slice(j * width, (j + 1) * width)
        total = nt(dq, wq_ref[part, :])
        total = total + tn(dkeys, wk_ref[:, part]) + tn(dvalues, wv_ref[:, part])
        scaled = total * (inverse * gain_ref[:, part].astype(F32))
        out_ref[j, :ROWS] = (scaled - x_ref[j, :ROWS].astype(F32) * along).astype(BF16)
        for saved_ref in refs[:-1]:
            out_ref[j, ROWS:] = saved_ref[0, 1, middle:]


def shifted(value, axis, steps):
    count = lax.axis_size(axis)
    first, last = (max(0, -steps), min(count, count - steps))
    return lax.ppermute(value, axis, [(source, source + steps) for source in range(first, last)])


def thirds(table):
    parts = []
    for _ in range(3):
        part = table.astype(ml_dtypes.bfloat16)
        parts.append(part)
        table = table - part.astype(np.float32)
    return jnp.asarray(np.stack(parts))


def rotation_tables():
    column = np.arange(HD)
    frequency = np.exp((column // 2).astype(np.float32) * np.float32(-2.0 * math.log(THETA) / HD))
    angles = np.arange(ROWS).astype(np.float32)[:, None] * frequency[None, :].astype(np.float32)
    parity = np.where(column % 2 == 0, -1.0, 1.0).astype(np.float32)
    cos = np.cos(angles).astype(np.float32)
    sin = (np.sin(angles) * parity).astype(np.float32)
    return [thirds(table) for table in (cos, sin, cos.T, sin.T)]


def per_device(
    saved,
    incoming,
    gain,
    w_query,
    w_key,
    w_value,
    w_out,
    seg_lengths,
    score_grad,
    rewards,
    sample_group,
    head_sample,
):
    tp_index = lax.axis_index("tp")
    tp_count = lax.axis_size("tp")
    last_section = lax.axis_index("pipe") == lax.axis_size("pipe") - 1
    share = tp_count // KV
    groups = [list(range(g * share, (g + 1) * share)) for g in range(KV)]
    wq, wk, wv, wo = w_query[0], w_key[0].T, w_value[0].T, w_out[0]
    kv_share = wk.shape[0]
    width = saved.shape[3]
    base = (tp_index // share * share).astype(jnp.int32)[None]
    place = (tp_index % share).astype(jnp.int32)[None]
    early, middle = FIRST_ROWS, FIRST_ROWS + MORE_ROWS
    tables = rotation_tables()

    def blocks_of(rows):
        return (jax.ShapeDtypeStruct((tp_count, rows, width), BF16),)

    def forward(tick, *rows):
        outs = (
            jax.ShapeDtypeStruct((ROWS, wq.shape[1]), BF16),
            jax.ShapeDtypeStruct((kv_share, 2 * ROWS), BF16),
            jax.ShapeDtypeStruct((ROWS, 1), F32),
            jax.ShapeDtypeStruct((ROWS, HD), F32),
            jax.ShapeDtypeStruct((ROWS, HD), F32),
            jax.ShapeDtypeStruct((kv_share, ROWS), F32),
            jax.ShapeDtypeStruct((kv_share, ROWS), F32),
        )
        return kernel_call(
            functools.partial(forward_body, tick),
            outs + (blocks_of(ROWS) if tick else ()),
            "s" + "v" * (9 + len(rows)),
            (place, seg_lengths, wq, wk, wv, gain, *tables, *rows),
        )

    def exchange(rows):
        return lax.all_to_all(rows, "tp", 0, 0)

    last_flag = last_section.astype(jnp.int32)[None]
    saved, base, place, last_flag = lax.optimization_barrier((saved, base, place, last_flag))
    (spread,) = kernel_call(spread_body, blocks_of(ROWS + early), "v", (saved,))
    first = exchange(spread)

    def chooser(received):
        return (last_flag, received, score_grad, rewards[None], sample_group[None], head_sample)

    grad = incoming[0]

    outputs = []
    for tick in range(TICKS):
        if tick == 0:
            pieces = forward(0, first)
            rows_full = first
            last = (saved,)
        else:
            rows_full = pieces[7]
            last = ()
        query, kv, inverse, cos, sin, cos_t, sin_t = pieces[:7]
        if tick == 0:
            (packed,) = kernel_call(
                functools.partial(first_pack_body, early),
                blocks_of(ROWS + kv_share + MORE_ROWS),
                "vvv",
                (grad, kv, saved),
            )
        else:
            grad, packed = kernel_call(
                functools.partial(turn_body, tick - 1),
                (jax.ShapeDtypeStruct(grad.shape, BF16),) + blocks_of(ROWS + kv_share),
                "s" + "v" * 6,
                (*chooser(received), kv),
            )
        got = exchange(packed)
        dquery, dkv, along = kernel_call(
            functools.partial(attention_body, tick),
            (
                jax.ShapeDtypeStruct(query.shape, BF16),
                jax.ShapeDtypeStruct((share, 2 * kv_share, ROWS), BF16),
                jax.ShapeDtypeStruct((ROWS, 1), F32),
            ),
            "s" + "v" * 6,
            (base, seg_lengths, got, wo, query, cos, sin),
        )
        dkv = lax.all_to_all(dkv, "tp", 0, 0, axis_index_groups=groups)
        (blocks,) = kernel_call(
            functools.partial(partial_body, middle),
            blocks_of(ROWS if tick else 2 * ROWS - middle),
            "v" * (11 + len(last)),
            (rows_full, dquery, dkv, wq, wk, wv, gain, inverse, along, cos_t, sin_t, *last),
        )
        blocks = exchange(blocks)
        total = jnp.sum(blocks[:, :ROWS].astype(F32), axis=0)
        result = (grad.astype(F32) + total).astype(BF16)
        received = shifted(result, "pipe", -1)
        if tick == 0:
            pieces = forward(1, first, got, blocks)
            received, pieces, result = lax.optimization_barrier((received, pieces, result))
        outputs.append(result)
    (carried,) = kernel_call(
        functools.partial(next_gradient, TICKS - 1),
        (jax.ShapeDtypeStruct(grad.shape, BF16),),
        "s" + "v" * 5,
        chooser(received),
    )
    return (jnp.stack(outputs, axis=0)[None], carried[None])


def solution(mesh):
    placed = (
        P("pipe", None, None, "tp"),
        P("pipe", None, "tp"),
        P("pipe", None),
        P("pipe", None, "tp"),
        P("pipe", None, "tp"),
        P("pipe", None, "tp"),
        P("pipe", "tp", None),
        P("pipe", None, None),
        P(None, None, "tp"),
        P(),
        P(),
        P(),
    )
    return jax.shard_map(
        per_device,
        mesh=mesh,
        in_specs=placed,
        out_specs=(P("pipe", None, None, "tp"), P("pipe", None, "tp")),
        check_vma=False,
    )
```

```python
import functools
import math

import jax
import jax.numpy as jnp
import ml_dtypes
import numpy as np
from jax import lax
from jax.experimental import pallas as pl
from jax.experimental.pallas import tpu as pltpu
from jax.sharding import PartitionSpec as P

D = 4096
KV = 4
HD = 128
ROWS = 128
TICKS = 2
GROUP_SIZE = 16
GROUPS = 32

EPS = 1e-05
THETA = 500000.0
SCALE = 1.0 / math.sqrt(HD)
F32 = jnp.float32
BF16 = jnp.bfloat16
VMEM_LIMIT = 16 * 1024 * 1024


def nn(a, b):
    return lax.dot_general(a, b, (((1,), (0,)), ((), ())), preferred_element_type=F32)


def nt(a, b):
    return lax.dot_general(a, b, (((1,), (1,)), ((), ())), preferred_element_type=F32)


def tn(a, b):
    return lax.dot_general(a, b, (((0,), (0,)), ((), ())), preferred_element_type=F32)


def pair_swap(v, axis):
    n = v.shape[axis]
    even = lax.broadcasted_iota(jnp.int32, v.shape, axis) % 2 == 0
    return jnp.where(even, pltpu.roll(v, n - 1, axis), pltpu.roll(v, 1, axis))


def kernel_call(body, outs, specs, args):
    vmem = pl.BlockSpec(memory_space=pltpu.VMEM)
    kinds = {
        "v": vmem,
        "s": pl.BlockSpec(memory_space=pltpu.SMEM),
    }
    return pl.pallas_call(
        body,
        out_shape=outs,
        in_specs=[kinds[kind] for kind in specs],
        out_specs=[vmem] * len(outs),
        compiler_params=pltpu.CompilerParams(vmem_limit_bytes=VMEM_LIMIT),
    )(*args)


def segment_starts(seg_ref, tick):
    lengths = seg_ref[0, tick : tick + 1, :].astype(F32)
    index = lax.broadcasted_iota(jnp.int32, lengths.shape, 1)
    return [
        jnp.sum(jnp.where(index < g, lengths, 0.0), axis=1, keepdims=True)
        for g in range(1, lengths.shape[1])
    ]


def iotas():
    row = lax.broadcasted_iota(jnp.int32, (ROWS, ROWS), 0).astype(F32)
    column = lax.broadcasted_iota(jnp.int32, (ROWS, ROWS), 1).astype(F32)
    return row, column


def position_match(seg_ref, tick):
    row, column = iotas()
    begin = jnp.zeros(row.shape, F32)
    for start in segment_starts(seg_ref, tick):
        begin = jnp.where(row >= start, start, begin)
    return jnp.where(column == row - begin, 1.0, 0.0).astype(BF16)


def spread_body(saved_ref, grad_ref, out_ref):
    for i in range(out_ref.shape[0]):
        for tick in range(TICKS):
            out_ref[i, tick * ROWS : (tick + 1) * ROWS] = saved_ref[0, tick]
        out_ref[i, TICKS * ROWS :] = grad_ref[0]


def forward_body(
    place_ref,
    seg_ref,
    wq_ref,
    wk_ref,
    wv_ref,
    gain_ref,
    ctab_ref,
    stab_ref,
    ctabt_ref,
    stabt_ref,
    x_ref,
    q_ref,
    kv_ref,
    inv_ref,
    cos_ref,
    sin_ref,
    cost_ref,
    sint_ref,
    wkv_ref,
):
    half = wk_ref.shape[0]
    wkv_ref[:half] = wk_ref[...]
    wkv_ref[half:] = wv_ref[...]
    blocks, _, width = x_ref.shape
    rows = TICKS * ROWS
    own = pl.ds(pl.multiple_of(place_ref[0] * half, half), half)
    squares = jnp.zeros((rows, width), F32)
    for j in range(blocks):
        xj = x_ref[j, :rows].astype(F32)
        squares = squares + xj * xj
    inverse = lax.rsqrt(jnp.sum(squares, axis=1, keepdims=True) * (1.0 / D) + EPS)
    query = jnp.zeros((rows, wq_ref.shape[1]), F32)
    kvt = jnp.zeros((2 * half, rows), F32)
    for j in range(blocks):
        part = slice(j * width, (j + 1) * width)
        normed = x_ref[j, :rows].astype(F32) * inverse * gain_ref[:, part].astype(F32)
        normed = normed.astype(BF16)
        query = query + nn(normed, wq_ref[part, :])
        kvt = kvt + nt(wkv_ref[:, part], normed)
    for tick in range(TICKS):
        here = slice(tick * ROWS, (tick + 1) * ROWS)
        inv_ref[tick] = inverse[here]
        match = position_match(seg_ref, tick)
        cos = sum(nn(match, ctab_ref[i]) for i in range(3))
        sin = sum(nn(match, stab_ref[i]) for i in range(3))
        cos_t = sum(nt(ctabt_ref[i, own, :], match) for i in range(3))
        sin_t = sum(nt(stabt_ref[i, own, :], match) for i in range(3))
        cos_ref[tick] = cos
        sin_ref[tick] = sin
        cost_ref[tick] = cos_t
        sint_ref[tick] = sin_t
        for h in range(query.shape[1] // HD):
            cols = slice(h * HD, (h + 1) * HD)
            head = query[here, cols]
            q_ref[tick, :, cols] = (head * cos + pair_swap(head, 1) * sin).astype(BF16)
        keys = kvt[:half, here]
        keys = keys * cos_t + pair_swap(keys, 0) * sin_t
        both = jnp.concatenate([keys, kvt[half:, here]], axis=0).astype(BF16)
        for i in range(kv_ref.shape[0]):
            kv_ref[i, tick] = both


def next_gradient(tick, last_ref, received_ref, score_ref, rewards_ref, group_ref, sample_ref, grad_ref):
    grad_ref[...] = received_ref[...]

    @pl.when(last_ref[0] > 0)
    def _():
        rewards = rewards_ref[...]
        samples = rewards.shape[1]
        prompt = lax.broadcasted_iota(jnp.int32, (GROUPS, samples), 0)
        member = prompt == group_ref[...]
        totals = jnp.sum(jnp.where(member, rewards, 0.0), axis=1, keepdims=True)
        own_total = jnp.sum(jnp.where(member, totals, 0.0), axis=0, keepdims=True)
        advantage = rewards - (own_total - rewards) / (GROUP_SIZE - 1)
        sample = lax.broadcasted_iota(jnp.int32, (ROWS, samples), 1)
        row, column = iotas()
        own = jnp.where(row == column, sample_ref[tick : tick + 1, :].astype(F32), 0.0)
        chosen = sample.astype(F32) == jnp.sum(own, axis=1, keepdims=True)
        row_adv = jnp.sum(jnp.where(chosen, advantage, 0.0), axis=1, keepdims=True)
        grad_ref[...] = (-row_adv * score_ref[tick].astype(F32)).astype(BF16)


def turn_body(
    tick,
    last_ref,
    received_ref,
    score_ref,
    rewards_ref,
    group_ref,
    sample_ref,
    grad_ref,
    out_ref,
):
    next_gradient(
        tick, last_ref, received_ref, score_ref, rewards_ref, group_ref, sample_ref, grad_ref
    )
    for i in range(out_ref.shape[0]):
        out_ref[i] = grad_ref[...]


def attention_body(
    tick, got_at, seg_ref, got_ref, wo_ref, q_ref, kv_ref, cos_ref, sin_ref, dq_ref, dkv_ref, t_ref
):
    blocks, _, width = got_ref.shape
    shares, half = dkv_ref.shape[0], dkv_ref.shape[1] // 2
    keys = jnp.concatenate([kv_ref[i, tick, :half] for i in range(shares)], axis=0)
    values = jnp.concatenate([kv_ref[i, tick, half:] for i in range(shares)], axis=0)
    cos = cos_ref[tick]
    sin = sin_ref[tick]
    row, column = iotas()
    allowed = column <= row
    for start in segment_starts(seg_ref, tick):
        allowed = allowed & ((row < start) | (column >= start))
    dout = jnp.zeros(dq_ref.shape, F32)
    for j in range(blocks):
        dout = dout + nt(got_ref[j, got_at : got_at + ROWS], wo_ref[:, j * width : (j + 1) * width])
    dout = dout.astype(BF16)
    dkeys = jnp.zeros((HD, ROWS), F32)
    dvalues = jnp.zeros((HD, ROWS), F32)
    own = jnp.zeros((ROWS, HD), F32)
    for h in range(dq_ref.shape[1] // HD):
        cols = slice(h * HD, (h + 1) * HD)
        query = q_ref[tick, :, cols]
        dhead = dout[:, cols]
        weights = jnp.where(allowed, jnp.exp(nn(query, keys) * SCALE), 0.0)
        softmax = weights / jnp.sum(weights, axis=1, keepdims=True)
        dprobs = nn(dhead, values)
        delta = jnp.sum(softmax * dprobs, axis=1, keepdims=True)
        dscores = (softmax * (dprobs - delta) * SCALE).astype(BF16)
        dquery = nt(dscores, keys)
        dkeys = dkeys + tn(query, dscores)
        dvalues = dvalues + tn(dhead, softmax.astype(BF16))
        own = own + dquery * query.astype(F32)
        dq_ref[:, cols] = (dquery * cos - pair_swap(dquery, 1) * sin).astype(BF16)
    shared = dkeys * keys.astype(F32) + dvalues * values.astype(F32)
    t_ref[...] = jnp.sum(own + shared.T, axis=1, keepdims=True)
    for i in range(shares):
        part = slice(i * half, (i + 1) * half)
        dkv_ref[i, :half] = dkeys[part].astype(BF16)
        dkv_ref[i, half:] = dvalues[part].astype(BF16)


def partial_body(
    tick,
    x_ref,
    dq_ref,
    dkv_ref,
    wq_ref,
    wkv_ref,
    gain_ref,
    inv_ref,
    t_ref,
    cost_ref,
    sint_ref,
    out_ref,
):
    blocks, _, width = out_ref.shape
    both = wkv_ref.shape[0]
    half = both // 2
    dkv = dkv_ref[0, :both].astype(F32)
    for i in range(1, dkv_ref.shape[0]):
        dkv = dkv + dkv_ref[i, :both].astype(F32)
    dkeys = dkv[:half]
    dkeys = dkeys * cost_ref[tick] - pair_swap(dkeys, 0) * sint_ref[tick]
    dkv = jnp.concatenate([dkeys, dkv[half:]], axis=0).T.astype(BF16)
    dq = dq_ref[...]
    inverse = inv_ref[tick]
    along = inverse * inverse * t_ref[...] * (1.0 / D)
    for j in range(blocks):
        part = slice(j * width, (j + 1) * width)
        total = nt(dq, wq_ref[part, :]) + nn(dkv, wkv_ref[:, part])
        scaled = total * (inverse * gain_ref[:, part].astype(F32))
        out_ref[j] = (scaled - x_ref[j, tick * ROWS : (tick + 1) * ROWS].astype(F32) * along).astype(BF16)


def shifted(value, axis, steps):
    count = lax.axis_size(axis)
    first, last = (max(0, -steps), min(count, count - steps))
    return lax.ppermute(value, axis, [(source, source + steps) for source in range(first, last)])


def thirds(table):
    parts = []
    for _ in range(3):
        part = table.astype(ml_dtypes.bfloat16)
        parts.append(part)
        table = table - part.astype(np.float32)
    return jnp.asarray(np.stack(parts))


def rotation_tables():
    column = np.arange(HD)
    frequency = np.exp((column // 2).astype(np.float32) * np.float32(-2.0 * math.log(THETA) / HD))
    angles = np.arange(ROWS).astype(np.float32)[:, None] * frequency[None, :].astype(np.float32)
    parity = np.where(column % 2 == 0, -1.0, 1.0).astype(np.float32)
    cos = np.cos(angles).astype(np.float32)
    sin = (np.sin(angles) * parity).astype(np.float32)
    return [thirds(table) for table in (cos, sin, cos.T, sin.T)]


def per_device(
    saved,
    incoming,
    gain,
    w_query,
    w_key,
    w_value,
    w_out,
    seg_lengths,
    score_grad,
    rewards,
    sample_group,
    head_sample,
):
    tp_index = lax.axis_index("tp")
    tp_count = lax.axis_size("tp")
    last_section = lax.axis_index("pipe") == lax.axis_size("pipe") - 1
    share = tp_count // KV
    groups = [list(range(g * share, (g + 1) * share)) for g in range(KV)]
    wq, wk, wv, wo = w_query[0], w_key[0].T, w_value[0].T, w_out[0]
    kv_share = wk.shape[0]
    width = saved.shape[3]
    place = (tp_index % share).astype(jnp.int32)[None]
    tables = rotation_tables()

    def blocks_of(rows):
        return (jax.ShapeDtypeStruct((tp_count, rows, width), BF16),)

    def exchange(rows):
        return lax.all_to_all(rows, "tp", 0, 0)

    last_flag = last_section.astype(jnp.int32)[None]
    saved, place, last_flag = lax.optimization_barrier((saved, place, last_flag))
    (spread,) = kernel_call(spread_body, blocks_of((TICKS + 1) * ROWS), "vv", (saved, incoming))
    first = exchange(spread)

    def chooser(received):
        return (last_flag, received, score_grad, rewards[None], sample_group[None], head_sample)

    grad = incoming[0]
    query, kv, inverse, cos, sin, cos_t, sin_t, wkv = kernel_call(
        forward_body,
        (
            jax.ShapeDtypeStruct((TICKS, ROWS, wq.shape[1]), BF16),
            jax.ShapeDtypeStruct((share, TICKS, 2 * kv_share, ROWS), BF16),
            jax.ShapeDtypeStruct((TICKS, ROWS, 1), F32),
            jax.ShapeDtypeStruct((TICKS, ROWS, HD), F32),
            jax.ShapeDtypeStruct((TICKS, ROWS, HD), F32),
            jax.ShapeDtypeStruct((TICKS, kv_share, ROWS), F32),
            jax.ShapeDtypeStruct((TICKS, kv_share, ROWS), F32),
            jax.ShapeDtypeStruct((2 * kv_share, wk.shape[1]), BF16),
        ),
        "s" + "v" * 10,
        (place, seg_lengths, wq, wk, wv, gain, *tables, first),
    )
    kv = lax.all_to_all(kv, "tp", 0, 0, axis_index_groups=groups)

    outputs = []
    for tick in range(TICKS):
        if tick == 0:
            got, got_at = first, TICKS * ROWS
        else:
            grad, packed = kernel_call(
                functools.partial(turn_body, tick - 1),
                (jax.ShapeDtypeStruct(grad.shape, BF16),) + blocks_of(ROWS),
                "s" + "v" * 5,
                chooser(received),
            )
            got, got_at = exchange(packed), 0
        dquery, dkv, along = kernel_call(
            functools.partial(attention_body, tick, got_at),
            (
                jax.ShapeDtypeStruct(query.shape[1:], BF16),
                jax.ShapeDtypeStruct((share, 2 * kv_share, ROWS), BF16),
                jax.ShapeDtypeStruct((ROWS, 1), F32),
            ),
            "v" * 7,
            (seg_lengths, got, wo, query, kv, cos, sin),
        )
        dkv = lax.all_to_all(dkv, "tp", 0, 0, axis_index_groups=groups)
        (blocks,) = kernel_call(
            functools.partial(partial_body, tick),
            blocks_of(ROWS),
            "v" * 10,
            (first, dquery, dkv, wq, wkv, gain, inverse, along, cos_t, sin_t),
        )
        blocks = exchange(blocks)
        total = jnp.sum(blocks.astype(F32), axis=0)
        result = (grad.astype(F32) + total).astype(BF16)
        received = shifted(result, "pipe", -1)
        if tick == 0:
            received, result = lax.optimization_barrier((received, result))
        outputs.append(result)
    (carried,) = kernel_call(
        functools.partial(next_gradient, TICKS - 1),
        (jax.ShapeDtypeStruct(grad.shape, BF16),),
        "s" + "v" * 5,
        chooser(received),
    )
    return (jnp.stack(outputs, axis=0)[None], carried[None])


def solution(mesh):
    placed = (
        P("pipe", None, None, "tp"),
        P("pipe", None, "tp"),
        P("pipe", None),
        P("pipe", None, "tp"),
        P("pipe", None, "tp"),
        P("pipe", None, "tp"),
        P("pipe", "tp", None),
        P("pipe", None, None),
        P(None, None, "tp"),
        P(),
        P(),
        P(),
    )
    return jax.shard_map(
        per_device,
        mesh=mesh,
        in_specs=placed,
        out_specs=(P("pipe", None, None, "tp"), P("pipe", None, "tp")),
        check_vma=False,
    )
```

```python
import functools
import math

import jax
import jax.numpy as jnp
import ml_dtypes
import numpy as np
from jax import lax
from jax.experimental import pallas as pl
from jax.experimental.pallas import tpu as pltpu
from jax.sharding import PartitionSpec as P

D = 4096
KV = 4
HD = 128
ROWS = 128
TICKS = 2
GROUP_SIZE = 16
GROUPS = 32

EPS = 1e-05
THETA = 500000.0
SCALE = 1.0 / math.sqrt(HD)
F32 = jnp.float32
BF16 = jnp.bfloat16
VMEM_LIMIT = 16 * 1024 * 1024


def nn(a, b):
    return lax.dot_general(a, b, (((1,), (0,)), ((), ())), preferred_element_type=F32)


def nt(a, b):
    return lax.dot_general(a, b, (((1,), (1,)), ((), ())), preferred_element_type=F32)


def tn(a, b):
    return lax.dot_general(a, b, (((0,), (0,)), ((), ())), preferred_element_type=F32)


def pair_swap(v, axis):
    n = v.shape[axis]
    even = lax.broadcasted_iota(jnp.int32, v.shape, axis) % 2 == 0
    return jnp.where(even, pltpu.roll(v, n - 1, axis), pltpu.roll(v, 1, axis))


def kernel_call(body, outs, specs, args):
    vmem = pl.BlockSpec(memory_space=pltpu.VMEM)
    kinds = {
        "v": vmem,
        "s": pl.BlockSpec(memory_space=pltpu.SMEM),
    }
    return pl.pallas_call(
        body,
        out_shape=outs,
        in_specs=[kinds[kind] for kind in specs],
        out_specs=[vmem] * len(outs),
        compiler_params=pltpu.CompilerParams(vmem_limit_bytes=VMEM_LIMIT),
    )(*args)


def segment_starts(seg_ref, tick):
    lengths = seg_ref[0, tick : tick + 1, :].astype(F32)
    index = lax.broadcasted_iota(jnp.int32, lengths.shape, 1)
    return [
        jnp.sum(jnp.where(index < g, lengths, 0.0), axis=1, keepdims=True)
        for g in range(1, lengths.shape[1])
    ]


def iotas():
    row = lax.broadcasted_iota(jnp.int32, (ROWS, ROWS), 0).astype(F32)
    column = lax.broadcasted_iota(jnp.int32, (ROWS, ROWS), 1).astype(F32)
    return row, column


def position_match(seg_ref, tick):
    row, column = iotas()
    begin = jnp.zeros(row.shape, F32)
    for start in segment_starts(seg_ref, tick):
        begin = jnp.where(row >= start, start, begin)
    return jnp.where(column == row - begin, 1.0, 0.0).astype(BF16)


def located(odd_ref, block, share):
    across = block % share * share + block // share
    return jnp.where(odd_ref[0] > 0, across, block)


def relay_body(got_ref, out_ref):
    for i in range(out_ref.shape[0]):
        out_ref[i] = got_ref[...]


def spread_body(saved_ref, grad_ref, out_ref):
    for i in range(out_ref.shape[0]):
        for tick in range(TICKS):
            out_ref[i, tick * ROWS : (tick + 1) * ROWS] = saved_ref[0, tick]
        out_ref[i, TICKS * ROWS :] = grad_ref[0]


def forward_body(
    place_ref,
    odd_ref,
    seg_ref,
    wq_ref,
    wk_ref,
    wv_ref,
    gain_ref,
    ctab_ref,
    stab_ref,
    ctabt_ref,
    stabt_ref,
    x_ref,
    q_ref,
    kv_ref,
    inv_ref,
    cos_ref,
    sin_ref,
    cost_ref,
    sint_ref,
    wkv_ref,
):
    half = wk_ref.shape[0]
    wkv_ref[:half] = wk_ref[...]
    wkv_ref[half:] = wv_ref[...]
    blocks, _, width = x_ref.shape
    rows = TICKS * ROWS
    own = pl.ds(pl.multiple_of(place_ref[0] * half, half), half)
    squares = jnp.zeros((rows, width), F32)
    for j in range(blocks):
        xj = x_ref[located(odd_ref, j, kv_ref.shape[0]), :rows].astype(F32)
        squares = squares + xj * xj
    inverse = lax.rsqrt(jnp.sum(squares, axis=1, keepdims=True) * (1.0 / D) + EPS)
    query = jnp.zeros((rows, wq_ref.shape[1]), F32)
    kvt = jnp.zeros((2 * half, rows), F32)
    for j in range(blocks):
        part = slice(j * width, (j + 1) * width)
        xj = x_ref[located(odd_ref, j, kv_ref.shape[0]), :rows].astype(F32)
        normed = xj * inverse * gain_ref[:, part].astype(F32)
        normed = normed.astype(BF16)
        query = query + nn(normed, wq_ref[part, :])
        kvt = kvt + nt(wkv_ref[:, part], normed)
    for tick in range(TICKS):
        here = slice(tick * ROWS, (tick + 1) * ROWS)
        inv_ref[tick] = inverse[here]
        match = position_match(seg_ref, tick)
        cos = sum(nn(match, ctab_ref[i]) for i in range(3))
        sin = sum(nn(match, stab_ref[i]) for i in range(3))
        cos_t = sum(nt(ctabt_ref[i, own, :], match) for i in range(3))
        sin_t = sum(nt(stabt_ref[i, own, :], match) for i in range(3))
        cos_ref[tick] = cos
        sin_ref[tick] = sin
        cost_ref[tick] = cos_t
        sint_ref[tick] = sin_t
        for h in range(query.shape[1] // HD):
            cols = slice(h * HD, (h + 1) * HD)
            head = query[here, cols]
            q_ref[tick, :, cols] = (head * cos + pair_swap(head, 1) * sin).astype(BF16)
        keys = kvt[:half, here]
        keys = keys * cos_t + pair_swap(keys, 0) * sin_t
        both = jnp.concatenate([keys, kvt[half:, here]], axis=0).astype(BF16)
        for i in range(kv_ref.shape[0]):
            kv_ref[i, tick] = both


def next_gradient(tick, last_ref, received_ref, score_ref, rewards_ref, group_ref, sample_ref, grad_ref):
    grad_ref[...] = received_ref[...]

    @pl.when(last_ref[0] > 0)
    def _():
        rewards = rewards_ref[...]
        samples = rewards.shape[1]
        prompt = lax.broadcasted_iota(jnp.int32, (GROUPS, samples), 0)
        member = prompt == group_ref[...]
        totals = jnp.sum(jnp.where(member, rewards, 0.0), axis=1, keepdims=True)
        own_total = jnp.sum(jnp.where(member, totals, 0.0), axis=0, keepdims=True)
        advantage = rewards - (own_total - rewards) / (GROUP_SIZE - 1)
        sample = lax.broadcasted_iota(jnp.int32, (ROWS, samples), 1)
        row, column = iotas()
        own = jnp.where(row == column, sample_ref[tick : tick + 1, :].astype(F32), 0.0)
        chosen = sample.astype(F32) == jnp.sum(own, axis=1, keepdims=True)
        row_adv = jnp.sum(jnp.where(chosen, advantage, 0.0), axis=1, keepdims=True)
        grad_ref[...] = (-row_adv * score_ref[tick].astype(F32)).astype(BF16)


def turn_body(
    tick,
    last_ref,
    received_ref,
    score_ref,
    rewards_ref,
    group_ref,
    sample_ref,
    grad_ref,
    out_ref,
):
    next_gradient(
        tick, last_ref, received_ref, score_ref, rewards_ref, group_ref, sample_ref, grad_ref
    )
    for i in range(out_ref.shape[0]):
        out_ref[i] = grad_ref[...]


def attention_body(
    tick, got_at, odd_ref, seg_ref, got_ref, wo_ref, q_ref, kv_ref, cos_ref, sin_ref, dq_ref, dkv_ref, t_ref
):
    blocks, _, width = got_ref.shape
    shares, half = dkv_ref.shape[0], dkv_ref.shape[1] // 2
    keys = jnp.concatenate([kv_ref[i, tick, :half] for i in range(shares)], axis=0)
    values = jnp.concatenate([kv_ref[i, tick, half:] for i in range(shares)], axis=0)
    cos = cos_ref[tick]
    sin = sin_ref[tick]
    row, column = iotas()
    allowed = column <= row
    for start in segment_starts(seg_ref, tick):
        allowed = allowed & ((row < start) | (column >= start))
    dout = jnp.zeros(dq_ref.shape, F32)
    for j in range(blocks):
        at = located(odd_ref, j, shares) if tick == 0 else j
        dout = dout + nt(
            got_ref[at, got_at : got_at + ROWS], wo_ref[:, j * width : (j + 1) * width])
    dout = dout.astype(BF16)
    dkeys = jnp.zeros((HD, ROWS), F32)
    dvalues = jnp.zeros((HD, ROWS), F32)
    own = jnp.zeros((ROWS, HD), F32)
    for h in range(dq_ref.shape[1] // HD):
        cols = slice(h * HD, (h + 1) * HD)
        query = q_ref[tick, :, cols]
        dhead = dout[:, cols]
        weights = jnp.where(allowed, jnp.exp(nn(query, keys) * SCALE), 0.0)
        softmax = weights / jnp.sum(weights, axis=1, keepdims=True)
        dprobs = nn(dhead, values)
        delta = jnp.sum(softmax * dprobs, axis=1, keepdims=True)
        dscores = (softmax * (dprobs - delta) * SCALE).astype(BF16)
        dquery = nt(dscores, keys)
        dkeys = dkeys + tn(query, dscores)
        dvalues = dvalues + tn(dhead, softmax.astype(BF16))
        own = own + dquery * query.astype(F32)
        dq_ref[:, cols] = (dquery * cos - pair_swap(dquery, 1) * sin).astype(BF16)
    shared = dkeys * keys.astype(F32) + dvalues * values.astype(F32)
    t_ref[...] = jnp.sum(own + shared.T, axis=1, keepdims=True)
    for i in range(shares):
        part = slice(i * half, (i + 1) * half)
        dkv_ref[i, :half] = dkeys[part].astype(BF16)
        dkv_ref[i, half:] = dvalues[part].astype(BF16)


def partial_body(
    tick,
    odd_ref,
    x_ref,
    dq_ref,
    dkv_ref,
    wq_ref,
    wkv_ref,
    gain_ref,
    inv_ref,
    t_ref,
    cost_ref,
    sint_ref,
    out_ref,
):
    blocks, _, width = out_ref.shape
    both = wkv_ref.shape[0]
    half = both // 2
    dkv = dkv_ref[0, :both].astype(F32)
    for i in range(1, dkv_ref.shape[0]):
        dkv = dkv + dkv_ref[i, :both].astype(F32)
    dkeys = dkv[:half]
    dkeys = dkeys * cost_ref[tick] - pair_swap(dkeys, 0) * sint_ref[tick]
    dkv = jnp.concatenate([dkeys, dkv[half:]], axis=0).T.astype(BF16)
    dq = dq_ref[...]
    inverse = inv_ref[tick]
    along = inverse * inverse * t_ref[...] * (1.0 / D)
    for j in range(blocks):
        part = slice(j * width, (j + 1) * width)
        total = nt(dq, wq_ref[part, :]) + nn(dkv, wkv_ref[:, part])
        scaled = total * (inverse * gain_ref[:, part].astype(F32))
        at = located(odd_ref, j, dkv_ref.shape[0])
        xj = x_ref[at, tick * ROWS : (tick + 1) * ROWS].astype(F32)
        out_ref[j] = (scaled - xj * along).astype(BF16)


def shifted(value, axis, steps):
    count = lax.axis_size(axis)
    first, last = (max(0, -steps), min(count, count - steps))
    return lax.ppermute(value, axis, [(source, source + steps) for source in range(first, last)])


def thirds(table):
    parts = []
    for _ in range(3):
        part = table.astype(ml_dtypes.bfloat16)
        parts.append(part)
        table = table - part.astype(np.float32)
    return jnp.asarray(np.stack(parts))


def rotation_tables():
    column = np.arange(HD)
    frequency = np.exp((column // 2).astype(np.float32) * np.float32(-2.0 * math.log(THETA) / HD))
    angles = np.arange(ROWS).astype(np.float32)[:, None] * frequency[None, :].astype(np.float32)
    parity = np.where(column % 2 == 0, -1.0, 1.0).astype(np.float32)
    cos = np.cos(angles).astype(np.float32)
    sin = (np.sin(angles) * parity).astype(np.float32)
    return [thirds(table) for table in (cos, sin, cos.T, sin.T)]


def per_device(
    saved,
    incoming,
    gain,
    w_query,
    w_key,
    w_value,
    w_out,
    seg_lengths,
    score_grad,
    rewards,
    sample_group,
    head_sample,
):
    tp_index = lax.axis_index("tp")
    tp_count = lax.axis_size("tp")
    last_section = lax.axis_index("pipe") == lax.axis_size("pipe") - 1
    share = tp_count // KV
    groups = [list(range(g * share, (g + 1) * share)) for g in range(KV)]
    wq, wk, wv, wo = w_query[0], w_key[0].T, w_value[0].T, w_out[0]
    kv_share = wk.shape[0]
    width = saved.shape[3]
    place = (tp_index % share).astype(jnp.int32)[None]
    tables = rotation_tables()

    def blocks_of(rows):
        return (jax.ShapeDtypeStruct((tp_count, rows, width), BF16),)

    def exchange(rows):
        return lax.all_to_all(rows, "tp", 0, 0)

    last_flag = last_section.astype(jnp.int32)[None]
    odd = (lax.axis_index("pipe") % 2).astype(jnp.int32)[None]
    saved, place, odd, last_flag = lax.optimization_barrier((saved, place, odd, last_flag))
    def stage(blocks, along):
        lines = []
        for section in range(lax.axis_size("pipe")):
            for line in range(share):
                chosen = [
                    line * share + i if (section + along) % 2 == 0 else i * share + line
                    for i in range(share)
                ]
                lines.append([section * tp_count + member for member in chosen])
        return lax.all_to_all(blocks, ("pipe", "tp"), 0, 0, axis_index_groups=lines)

    rows_in = (TICKS + 1) * ROWS
    (spread,) = kernel_call(
        spread_body,
        (jax.ShapeDtypeStruct((share, rows_in, width), BF16),),
        "vv",
        (saved, incoming),
    )
    (relay,) = kernel_call(
        relay_body,
        (jax.ShapeDtypeStruct((share, share, rows_in, width), BF16),),
        "v",
        (stage(spread, 0),),
    )
    first = stage(relay, 1).reshape(tp_count, rows_in, width)

    def chooser(received):
        return (last_flag, received, score_grad, rewards[None], sample_group[None], head_sample)

    grad = incoming[0]
    query, kv, inverse, cos, sin, cos_t, sin_t, wkv = kernel_call(
        forward_body,
        (
            jax.ShapeDtypeStruct((TICKS, ROWS, wq.shape[1]), BF16),
            jax.ShapeDtypeStruct((share, TICKS, 2 * kv_share, ROWS), BF16),
            jax.ShapeDtypeStruct((TICKS, ROWS, 1), F32),
            jax.ShapeDtypeStruct((TICKS, ROWS, HD), F32),
            jax.ShapeDtypeStruct((TICKS, ROWS, HD), F32),
            jax.ShapeDtypeStruct((TICKS, kv_share, ROWS), F32),
            jax.ShapeDtypeStruct((TICKS, kv_share, ROWS), F32),
            jax.ShapeDtypeStruct((2 * kv_share, wk.shape[1]), BF16),
        ),
        "ss" + "v" * 10,
        (place, odd, seg_lengths, wq, wk, wv, gain, *tables, first),
    )
    kv = lax.all_to_all(kv, "tp", 0, 0, axis_index_groups=groups)

    outputs = []
    for tick in range(TICKS):
        if tick == 0:
            got, got_at = first, TICKS * ROWS
        else:
            grad, packed = kernel_call(
                functools.partial(turn_body, tick - 1),
                (jax.ShapeDtypeStruct(grad.shape, BF16),) + blocks_of(ROWS),
                "s" + "v" * 5,
                chooser(received),
            )
            got, got_at = exchange(packed), 0
        dquery, dkv, along = kernel_call(
            functools.partial(attention_body, tick, got_at),
            (
                jax.ShapeDtypeStruct(query.shape[1:], BF16),
                jax.ShapeDtypeStruct((share, 2 * kv_share, ROWS), BF16),
                jax.ShapeDtypeStruct((ROWS, 1), F32),
            ),
            "s" + "v" * 7,
            (odd, seg_lengths, got, wo, query, kv, cos, sin),
        )
        dkv = lax.all_to_all(dkv, "tp", 0, 0, axis_index_groups=groups)
        (blocks,) = kernel_call(
            functools.partial(partial_body, tick),
            blocks_of(ROWS),
            "s" + "v" * 10,
            (odd, first, dquery, dkv, wq, wkv, gain, inverse, along, cos_t, sin_t),
        )
        blocks = exchange(blocks)
        total = jnp.sum(blocks.astype(F32), axis=0)
        result = (grad.astype(F32) + total).astype(BF16)
        received = shifted(result, "pipe", -1)
        if tick == 0:
            received, result = lax.optimization_barrier((received, result))
        outputs.append(result)
    (carried,) = kernel_call(
        functools.partial(next_gradient, TICKS - 1),
        (jax.ShapeDtypeStruct(grad.shape, BF16),),
        "s" + "v" * 5,
        chooser(received),
    )
    return (jnp.stack(outputs, axis=0)[None], carried[None])


def solution(mesh):
    placed = (
        P("pipe", None, None, "tp"),
        P("pipe", None, "tp"),
        P("pipe", None),
        P("pipe", None, "tp"),
        P("pipe", None, "tp"),
        P("pipe", None, "tp"),
        P("pipe", "tp", None),
        P("pipe", None, None),
        P(None, None, "tp"),
        P(),
        P(),
        P(),
    )
    return jax.shard_map(
        per_device,
        mesh=mesh,
        in_specs=placed,
        out_specs=(P("pipe", None, None, "tp"), P("pipe", None, "tp")),
        check_vma=False,
    )
```

```python
import functools
import math

import jax
import jax.numpy as jnp
import ml_dtypes
import numpy as np
from jax import lax
from jax.experimental import pallas as pl
from jax.experimental.pallas import tpu as pltpu
from jax.sharding import PartitionSpec as P

D = 4096
KV = 4
HD = 128
ROWS = 128
TICKS = 2
GROUP_SIZE = 16
GROUPS = 32

EPS = 1e-05
THETA = 500000.0
SCALE = 1.0 / math.sqrt(HD)
F32 = jnp.float32
BF16 = jnp.bfloat16
VMEM_LIMIT = 16 * 1024 * 1024


def nn(a, b):
    return lax.dot_general(a, b, (((1,), (0,)), ((), ())), preferred_element_type=F32)


def nt(a, b):
    return lax.dot_general(a, b, (((1,), (1,)), ((), ())), preferred_element_type=F32)


def tn(a, b):
    return lax.dot_general(a, b, (((0,), (0,)), ((), ())), preferred_element_type=F32)


def pair_swap(v, axis):
    n = v.shape[axis]
    even = lax.broadcasted_iota(jnp.int32, v.shape, axis) % 2 == 0
    return jnp.where(even, pltpu.roll(v, n - 1, axis), pltpu.roll(v, 1, axis))


def kernel_call(body, outs, specs, args):
    vmem = pl.BlockSpec(memory_space=pltpu.VMEM)
    kinds = {
        "v": vmem,
        "s": pl.BlockSpec(memory_space=pltpu.SMEM),
    }
    return pl.pallas_call(
        body,
        out_shape=outs,
        in_specs=[kinds[kind] for kind in specs],
        out_specs=[vmem] * len(outs),
        compiler_params=pltpu.CompilerParams(vmem_limit_bytes=VMEM_LIMIT),
    )(*args)


def segment_starts(seg_ref, tick):
    lengths = seg_ref[0, tick : tick + 1, :].astype(F32)
    index = lax.broadcasted_iota(jnp.int32, lengths.shape, 1)
    return [
        jnp.sum(jnp.where(index < g, lengths, 0.0), axis=1, keepdims=True)
        for g in range(1, lengths.shape[1])
    ]


def iotas():
    row = lax.broadcasted_iota(jnp.int32, (ROWS, ROWS), 0).astype(F32)
    column = lax.broadcasted_iota(jnp.int32, (ROWS, ROWS), 1).astype(F32)
    return row, column


def position_match(seg_ref, tick):
    row, column = iotas()
    begin = jnp.zeros(row.shape, F32)
    for start in segment_starts(seg_ref, tick):
        begin = jnp.where(row >= start, start, begin)
    return jnp.where(column == row - begin, 1.0, 0.0).astype(BF16)


def located(odd_ref, block, share):
    across = block % share * share + block // share
    return jnp.where(odd_ref[0] > 0, across, block)


def relay_body(got_ref, out_ref):
    for i in range(out_ref.shape[0]):
        out_ref[i] = got_ref[...]


def spread_body(rows_ref, out_ref):
    for i in range(out_ref.shape[0]):
        out_ref[i] = rows_ref[...]


def rotate_heads(query, cos, sin, q_ref):
    for h in range(query.shape[1] // HD):
        cols = slice(h * HD, (h + 1) * HD)
        head = query[:, cols]
        q_ref[:, cols] = (head * cos + pair_swap(head, 1) * sin).astype(BF16)


def forward_body(
    place_ref,
    odd_ref,
    seg_ref,
    wq_ref,
    wk_ref,
    wv_ref,
    gain_ref,
    ctab_ref,
    stab_ref,
    ctabt_ref,
    stabt_ref,
    x_ref,
    q_ref,
    kv_ref,
    inv_ref,
    cos_ref,
    sin_ref,
    cost_ref,
    sint_ref,
    wkv_ref,
):
    half = wk_ref.shape[0]
    wkv_ref[:half] = wk_ref[...]
    wkv_ref[half:] = wv_ref[...]
    blocks, _, width = x_ref.shape
    rows = TICKS * ROWS
    q_rows = ROWS
    own = pl.ds(pl.multiple_of(place_ref[0] * half, half), half)
    squares = jnp.zeros((rows, width), F32)
    query = jnp.zeros((q_rows, wq_ref.shape[1]), F32)
    kvt = jnp.zeros((2 * half, rows), F32)
    for j in range(blocks):
        part = slice(j * width, (j + 1) * width)
        xj = x_ref[located(odd_ref, j, kv_ref.shape[0]), :rows].astype(F32)
        squares = squares + xj * xj
        gained = (xj * gain_ref[:, part].astype(F32)).astype(BF16)
        query = query + nn(gained[:q_rows], wq_ref[part, :])
        kvt = kvt + nt(wkv_ref[:, part], gained)
    inverse = lax.rsqrt(jnp.sum(squares, axis=1, keepdims=True) * (1.0 / D) + EPS)
    eye = lax.broadcasted_iota(jnp.int32, (rows, rows), 0) == lax.broadcasted_iota(
        jnp.int32, (rows, rows), 1
    )
    kvt = kvt * jnp.sum(jnp.where(eye, inverse, 0.0), axis=0, keepdims=True)
    query = query * inverse[:q_rows]
    for tick in range(TICKS):
        here = slice(tick * ROWS, (tick + 1) * ROWS)
        inv_ref[tick] = inverse[here]
        match = position_match(seg_ref, tick)
        cos = sum(nn(match, ctab_ref[i]) for i in range(3))
        sin = sum(nn(match, stab_ref[i]) for i in range(3))
        cos_t = sum(nt(ctabt_ref[i, own, :], match) for i in range(3))
        sin_t = sum(nt(stabt_ref[i, own, :], match) for i in range(3))
        cos_ref[tick] = cos
        sin_ref[tick] = sin
        cost_ref[tick] = cos_t
        sint_ref[tick] = sin_t
        if tick == 0:
            rotate_heads(query, cos, sin, q_ref)
        keys = kvt[:half, here]
        keys = keys * cos_t + pair_swap(keys, 0) * sin_t
        both = jnp.concatenate([keys, kvt[half:, here]], axis=0).astype(BF16)
        for i in range(kv_ref.shape[0]):
            kv_ref[i, tick] = both


def next_gradient(tick, last_ref, received_ref, score_ref, rewards_ref, group_ref, sample_ref, grad_ref):
    grad_ref[...] = received_ref[...]

    @pl.when(last_ref[0] > 0)
    def _():
        rewards = rewards_ref[...]
        samples = rewards.shape[1]
        prompt = lax.broadcasted_iota(jnp.int32, (GROUPS, samples), 0)
        member = prompt == group_ref[...]
        totals = jnp.sum(jnp.where(member, rewards, 0.0), axis=1, keepdims=True)
        own_total = jnp.sum(jnp.where(member, totals, 0.0), axis=0, keepdims=True)
        advantage = rewards - (own_total - rewards) / (GROUP_SIZE - 1)
        sample = lax.broadcasted_iota(jnp.int32, (ROWS, samples), 1)
        row, column = iotas()
        own = jnp.where(row == column, sample_ref[tick : tick + 1, :].astype(F32), 0.0)
        chosen = sample.astype(F32) == jnp.sum(own, axis=1, keepdims=True)
        row_adv = jnp.sum(jnp.where(chosen, advantage, 0.0), axis=1, keepdims=True)
        grad_ref[...] = (-row_adv * score_ref[tick].astype(F32)).astype(BF16)


def turn_body(
    tick,
    last_ref,
    received_ref,
    score_ref,
    rewards_ref,
    group_ref,
    sample_ref,
    grad_ref,
    out_ref,
):
    next_gradient(
        tick, last_ref, received_ref, score_ref, rewards_ref, group_ref, sample_ref, grad_ref
    )
    for i in range(out_ref.shape[0]):
        out_ref[i] = grad_ref[...]


def softmaxes(tick, seg_ref, q_ref, keys):
    row, column = iotas()
    allowed = column <= row
    for start in segment_starts(seg_ref, tick):
        allowed = allowed & ((row < start) | (column >= start))
    out = []
    for h in range(q_ref.shape[1] // HD):
        query = q_ref[:, h * HD : (h + 1) * HD]
        weights = jnp.where(allowed, jnp.exp(nn(query, keys) * SCALE), 0.0)
        out.append(weights / jnp.sum(weights, axis=1, keepdims=True))
    return out


def query_body(
    tick,
    odd_ref,
    seg_ref,
    wq_ref,
    gain_ref,
    x_ref,
    kv_ref,
    inv_ref,
    cos_ref,
    sin_ref,
    q_ref,
    soft_ref,
):
    blocks, _, width = x_ref.shape
    shares, half = kv_ref.shape[0], kv_ref.shape[2] // 2
    here = slice(tick * ROWS, (tick + 1) * ROWS)
    query = jnp.zeros(q_ref.shape, F32)
    for j in range(blocks):
        part = slice(j * width, (j + 1) * width)
        xj = x_ref[located(odd_ref, j, shares), here].astype(F32)
        gained = (xj * gain_ref[:, part].astype(F32)).astype(BF16)
        query = query + nn(gained, wq_ref[part, :])
    rotate_heads(query * inv_ref[tick], cos_ref[tick], sin_ref[tick], q_ref)
    keys = jnp.concatenate([kv_ref[i, tick, :half] for i in range(shares)], axis=0)
    for h, softmax in enumerate(softmaxes(tick, seg_ref, q_ref, keys)):
        soft_ref[h] = softmax


def attention_body(
    tick,
    got_at,
    odd_ref,
    seg_ref,
    got_ref,
    wo_ref,
    q_ref,
    kv_ref,
    cos_ref,
    sin_ref,
    *refs,
):
    *ready, dq_ref, dkv_ref, t_ref = refs
    blocks, _, width = got_ref.shape
    shares, half = dkv_ref.shape[0], dkv_ref.shape[1] // 2
    keys = jnp.concatenate([kv_ref[i, tick, :half] for i in range(shares)], axis=0)
    values = jnp.concatenate([kv_ref[i, tick, half:] for i in range(shares)], axis=0)
    cos = cos_ref[tick]
    sin = sin_ref[tick]
    if ready:
        soft = [ready[0][h] for h in range(ready[0].shape[0])]
    else:
        soft = softmaxes(tick, seg_ref, q_ref, keys)
    dout = jnp.zeros(dq_ref.shape, F32)
    for j in range(blocks):
        at = located(odd_ref, j, shares) if tick == 0 else j
        dout = dout + nt(
            got_ref[at, got_at : got_at + ROWS], wo_ref[:, j * width : (j + 1) * width])
    dout = dout.astype(BF16)
    dkeys = jnp.zeros((HD, ROWS), F32)
    dvalues = jnp.zeros((HD, ROWS), F32)
    own = jnp.zeros((ROWS, HD), F32)
    for h in range(dq_ref.shape[1] // HD):
        cols = slice(h * HD, (h + 1) * HD)
        query = q_ref[:, cols]
        dhead = dout[:, cols]
        softmax = soft[h]
        dprobs = nn(dhead, values)
        delta = jnp.sum(softmax * dprobs, axis=1, keepdims=True)
        dscores = (softmax * (dprobs - delta) * SCALE).astype(BF16)
        dquery = nt(dscores, keys)
        dkeys = dkeys + tn(query, dscores)
        dvalues = dvalues + tn(dhead, softmax.astype(BF16))
        own = own + dquery * query.astype(F32)
        dq_ref[:, cols] = (dquery * cos - pair_swap(dquery, 1) * sin).astype(BF16)
    shared = dkeys * keys.astype(F32) + dvalues * values.astype(F32)
    t_ref[...] = jnp.sum(own + shared.T, axis=1, keepdims=True)
    for i in range(shares):
        part = slice(i * half, (i + 1) * half)
        dkv_ref[i, :half] = dkeys[part].astype(BF16)
        dkv_ref[i, half:] = dvalues[part].astype(BF16)


def partial_body(
    tick,
    odd_ref,
    x_ref,
    dq_ref,
    dkv_ref,
    wq_ref,
    wkv_ref,
    gain_ref,
    inv_ref,
    t_ref,
    cost_ref,
    sint_ref,
    out_ref,
):
    blocks, _, width = out_ref.shape
    both = wkv_ref.shape[0]
    half = both // 2
    dkv = dkv_ref[0, :both].astype(F32)
    for i in range(1, dkv_ref.shape[0]):
        dkv = dkv + dkv_ref[i, :both].astype(F32)
    dkeys = dkv[:half]
    dkeys = dkeys * cost_ref[tick] - pair_swap(dkeys, 0) * sint_ref[tick]
    dkv = jnp.concatenate([dkeys, dkv[half:]], axis=0).T.astype(BF16)
    dq = dq_ref[...]
    inverse = inv_ref[tick]
    along = inverse * inverse * t_ref[...] * (1.0 / D)
    for j in range(blocks):
        part = slice(j * width, (j + 1) * width)
        total = nt(dq, wq_ref[part, :]) + nn(dkv, wkv_ref[:, part])
        scaled = total * (inverse * gain_ref[:, part].astype(F32))
        at = located(odd_ref, j, dkv_ref.shape[0])
        xj = x_ref[at, tick * ROWS : (tick + 1) * ROWS].astype(F32)
        out_ref[j] = (scaled - xj * along).astype(BF16)


def shifted(value, axis, steps):
    count = lax.axis_size(axis)
    first, last = (max(0, -steps), min(count, count - steps))
    return lax.ppermute(value, axis, [(source, source + steps) for source in range(first, last)])


def thirds(table):
    parts = []
    for _ in range(3):
        part = table.astype(ml_dtypes.bfloat16)
        parts.append(part)
        table = table - part.astype(np.float32)
    return jnp.asarray(np.stack(parts))


def rotation_tables():
    column = np.arange(HD)
    frequency = np.exp((column // 2).astype(np.float32) * np.float32(-2.0 * math.log(THETA) / HD))
    angles = np.arange(ROWS).astype(np.float32)[:, None] * frequency[None, :].astype(np.float32)
    parity = np.where(column % 2 == 0, -1.0, 1.0).astype(np.float32)
    cos = np.cos(angles).astype(np.float32)
    sin = (np.sin(angles) * parity).astype(np.float32)
    return [thirds(table) for table in (cos, sin, cos.T, sin.T)]


def per_device(
    saved,
    incoming,
    gain,
    w_query,
    w_key,
    w_value,
    w_out,
    seg_lengths,
    score_grad,
    rewards,
    sample_group,
    head_sample,
):
    tp_index = lax.axis_index("tp")
    tp_count = lax.axis_size("tp")
    last_section = lax.axis_index("pipe") == lax.axis_size("pipe") - 1
    share = tp_count // KV
    groups = [list(range(g * share, (g + 1) * share)) for g in range(KV)]
    wq, wk, wv, wo = w_query[0], w_key[0].T, w_value[0].T, w_out[0]
    kv_share = wk.shape[0]
    width = saved.shape[3]
    place = (tp_index & (share - 1)).astype(jnp.int32)[None]
    tables = rotation_tables()

    def blocks_of(rows):
        return (jax.ShapeDtypeStruct((tp_count, rows, width), BF16),)

    def exchange(rows):
        return lax.all_to_all(rows, "tp", 0, 0)

    last_flag = last_section.astype(jnp.int32)[None]
    odd = (lax.axis_index("pipe") & 1).astype(jnp.int32)[None]
    saved, place, odd, last_flag = lax.optimization_barrier((saved, place, odd, last_flag))
    def stage(blocks, along):
        lines = []
        for section in range(lax.axis_size("pipe")):
            for line in range(share):
                chosen = [
                    line * share + i if (section + along) % 2 == 0 else i * share + line
                    for i in range(share)
                ]
                lines.append([section * tp_count + member for member in chosen])
        return lax.all_to_all(blocks, ("pipe", "tp"), 0, 0, axis_index_groups=lines)

    rows_in = (TICKS + 1) * ROWS
    (spread,) = kernel_call(
        spread_body,
        (jax.ShapeDtypeStruct((share, rows_in, width), BF16),),
        "v",
        (jnp.concatenate([saved[0].reshape(TICKS * ROWS, width), incoming[0]], axis=0),),
    )
    (relay,) = kernel_call(
        relay_body,
        (jax.ShapeDtypeStruct((share, share, rows_in, width), BF16),),
        "v",
        (stage(spread, 0),),
    )
    first = stage(relay, 1).reshape(tp_count, rows_in, width)

    def chooser(received):
        return (last_flag, received, score_grad, rewards[None], sample_group[None], head_sample)

    grad = incoming[0]
    query, kv, inverse, cos, sin, cos_t, sin_t, wkv = kernel_call(
        forward_body,
        (
            jax.ShapeDtypeStruct((ROWS, wq.shape[1]), BF16),
            jax.ShapeDtypeStruct((share, TICKS, 2 * kv_share, ROWS), BF16),
            jax.ShapeDtypeStruct((TICKS, ROWS, 1), F32),
            jax.ShapeDtypeStruct((TICKS, ROWS, HD), F32),
            jax.ShapeDtypeStruct((TICKS, ROWS, HD), F32),
            jax.ShapeDtypeStruct((TICKS, kv_share, ROWS), F32),
            jax.ShapeDtypeStruct((TICKS, kv_share, ROWS), F32),
            jax.ShapeDtypeStruct((2 * kv_share, wk.shape[1]), BF16),
        ),
        "ss" + "v" * 10,
        (place, odd, seg_lengths, wq, wk, wv, gain, *tables, first),
    )
    kv = lax.all_to_all(kv, "tp", 0, 0, axis_index_groups=groups)

    ready = []
    outputs = []
    for tick in range(TICKS):
        if tick == 0:
            got, got_at = first, TICKS * ROWS
        else:
            grad, packed = kernel_call(
                functools.partial(turn_body, tick - 1),
                (jax.ShapeDtypeStruct(grad.shape, BF16),) + blocks_of(ROWS),
                "s" + "v" * 5,
                chooser(received),
            )
            got, got_at = exchange(packed), 0
        dquery, dkv, along = kernel_call(
            functools.partial(attention_body, tick, got_at),
            (
                jax.ShapeDtypeStruct(query.shape, BF16),
                jax.ShapeDtypeStruct((share, 2 * kv_share, ROWS), BF16),
                jax.ShapeDtypeStruct((ROWS, 1), F32),
            ),
            "s" + "v" * (7 + len(ready)),
            (odd, seg_lengths, got, wo, query, kv, cos, sin, *ready),
        )
        dkv = lax.all_to_all(dkv, "tp", 0, 0, axis_index_groups=groups)
        (blocks,) = kernel_call(
            functools.partial(partial_body, tick),
            blocks_of(ROWS),
            "s" + "v" * 10,
            (odd, first, dquery, dkv, wq, wkv, gain, inverse, along, cos_t, sin_t),
        )
        blocks = exchange(blocks)
        if tick == 0:
            blocks, inverse = lax.optimization_barrier((blocks, inverse))
        total = jnp.sum(blocks.astype(F32), axis=0)
        result = (grad.astype(F32) + total).astype(BF16)
        received = shifted(result, "pipe", -1)
        if tick == 0:
            later = kernel_call(
                functools.partial(query_body, 1),
                (
                    jax.ShapeDtypeStruct(query.shape, BF16),
                    jax.ShapeDtypeStruct((query.shape[1] // HD, ROWS, ROWS), F32),
                ),
                "s" + "v" * 8,
                (odd, seg_lengths, wq, gain, first, kv, inverse, cos, sin),
            )
            received, result, later = lax.optimization_barrier((received, result, later))
            query, *ready = later
        outputs.append(result)
    (carried,) = kernel_call(
        functools.partial(next_gradient, TICKS - 1),
        (jax.ShapeDtypeStruct(grad.shape, BF16),),
        "s" + "v" * 5,
        chooser(received),
    )
    return (jnp.stack(outputs, axis=0)[None], carried[None])


def solution(mesh):
    placed = (
        P("pipe", None, None, "tp"),
        P("pipe", None, "tp"),
        P("pipe", None),
        P("pipe", None, "tp"),
        P("pipe", None, "tp"),
        P("pipe", None, "tp"),
        P("pipe", "tp", None),
        P("pipe", None, None),
        P(None, None, "tp"),
        P(),
        P(),
        P(),
    )
    return jax.shard_map(
        per_device,
        mesh=mesh,
        in_specs=placed,
        out_specs=(P("pipe", None, None, "tp"), P("pipe", None, "tp")),
        check_vma=False,
    )
```

```python
import functools
import math

import jax
import jax.numpy as jnp
import ml_dtypes
import numpy as np
from jax import lax
from jax.experimental import pallas as pl
from jax.experimental.pallas import tpu as pltpu
from jax.sharding import PartitionSpec as P

D = 4096
KV = 4
HD = 128
ROWS = 128
TICKS = 2
GROUP_SIZE = 16
GROUPS = 32

EPS = 1e-05
THETA = 500000.0
SCALE = 1.0 / math.sqrt(HD)
F32 = jnp.float32
BF16 = jnp.bfloat16
VMEM_LIMIT = 16 * 1024 * 1024


def nn(a, b):
    return lax.dot_general(a, b, (((1,), (0,)), ((), ())), preferred_element_type=F32)


def nt(a, b):
    return lax.dot_general(a, b, (((1,), (1,)), ((), ())), preferred_element_type=F32)


def tn(a, b):
    return lax.dot_general(a, b, (((0,), (0,)), ((), ())), preferred_element_type=F32)


def pair_swap(v, axis):
    n = v.shape[axis]
    even = lax.broadcasted_iota(jnp.int32, v.shape, axis) % 2 == 0
    return jnp.where(even, pltpu.roll(v, n - 1, axis), pltpu.roll(v, 1, axis))


def kernel_call(body, outs, specs, args):
    vmem = pl.BlockSpec(memory_space=pltpu.VMEM)
    kinds = {
        "v": vmem,
        "s": pl.BlockSpec(memory_space=pltpu.SMEM),
    }
    return pl.pallas_call(
        body,
        out_shape=outs,
        in_specs=[kinds[kind] for kind in specs],
        out_specs=[vmem] * len(outs),
        compiler_params=pltpu.CompilerParams(vmem_limit_bytes=VMEM_LIMIT),
    )(*args)


def segment_starts(seg_ref, tick):
    lengths = seg_ref[0, tick : tick + 1, :].astype(F32)
    index = lax.broadcasted_iota(jnp.int32, lengths.shape, 1)
    return [
        jnp.sum(jnp.where(index < g, lengths, 0.0), axis=1, keepdims=True)
        for g in range(1, lengths.shape[1])
    ]


def iotas():
    row = lax.broadcasted_iota(jnp.int32, (ROWS, ROWS), 0).astype(F32)
    column = lax.broadcasted_iota(jnp.int32, (ROWS, ROWS), 1).astype(F32)
    return row, column


def position_match(seg_ref, tick):
    row, column = iotas()
    begin = jnp.zeros(row.shape, F32)
    for start in segment_starts(seg_ref, tick):
        begin = jnp.where(row >= start, start, begin)
    return jnp.where(column == row - begin, 1.0, 0.0).astype(BF16)


def located(odd_ref, block, share):
    across = block % share * share + block // share
    return jnp.where(odd_ref[0] > 0, across, block)


def relay_body(
    first_ref, got_ref, score_ref, rewards_ref, group_ref, sample_ref, out_ref, head_ref
):
    @pl.when(first_ref[0] > 0)
    def _():
        head_rows(score_ref, rewards_ref, group_ref, sample_ref, head_ref)

    for i in range(out_ref.shape[0]):
        out_ref[i] = got_ref[...]


def spread_body(rows_ref, out_ref):
    for i in range(out_ref.shape[0]):
        out_ref[i] = rows_ref[...]


def rotate_heads(query, cos, sin, q_ref):
    for h in range(query.shape[1] // HD):
        cols = slice(h * HD, (h + 1) * HD)
        head = query[:, cols]
        q_ref[:, cols] = (head * cos + pair_swap(head, 1) * sin).astype(BF16)


def forward_body(
    place_ref,
    odd_ref,
    seg_ref,
    wq_ref,
    wk_ref,
    wv_ref,
    gain_ref,
    ctab_ref,
    stab_ref,
    ctabt_ref,
    stabt_ref,
    x_ref,
    q_ref,
    kv_ref,
    inv_ref,
    cos_ref,
    sin_ref,
    cost_ref,
    sint_ref,
    wkv_ref,
):
    half = wk_ref.shape[0]
    wkv_ref[:half] = wk_ref[...]
    wkv_ref[half:] = wv_ref[...]
    blocks, _, width = x_ref.shape
    rows = TICKS * ROWS
    q_rows = ROWS
    own = pl.ds(pl.multiple_of(place_ref[0] * half, half), half)
    squares = jnp.zeros((rows, width), F32)
    query = jnp.zeros((q_rows, wq_ref.shape[1]), F32)
    kvt = jnp.zeros((2 * half, rows), F32)
    for j in range(blocks):
        part = slice(j * width, (j + 1) * width)
        xj = x_ref[located(odd_ref, j, kv_ref.shape[0]), :rows].astype(F32)
        squares = squares + xj * xj
        gained = (xj * gain_ref[:, part].astype(F32)).astype(BF16)
        query = query + nn(gained[:q_rows], wq_ref[part, :])
        kvt = kvt + nt(wkv_ref[:, part], gained)
    inverse = lax.rsqrt(jnp.sum(squares, axis=1, keepdims=True) * (1.0 / D) + EPS)
    eye = lax.broadcasted_iota(jnp.int32, (rows, rows), 0) == lax.broadcasted_iota(
        jnp.int32, (rows, rows), 1
    )
    kvt = kvt * jnp.sum(jnp.where(eye, inverse, 0.0), axis=0, keepdims=True)
    query = query * inverse[:q_rows]
    for tick in range(TICKS):
        here = slice(tick * ROWS, (tick + 1) * ROWS)
        inv_ref[tick] = inverse[here]
        match = position_match(seg_ref, tick)
        cos = sum(nn(match, ctab_ref[i]) for i in range(3))
        sin = sum(nn(match, stab_ref[i]) for i in range(3))
        cos_t = sum(nt(ctabt_ref[i, own, :], match) for i in range(3))
        sin_t = sum(nt(stabt_ref[i, own, :], match) for i in range(3))
        cos_ref[tick] = cos
        sin_ref[tick] = sin
        cost_ref[tick] = cos_t
        sint_ref[tick] = sin_t
        if tick == 0:
            rotate_heads(query, cos, sin, q_ref)
        keys = kvt[:half, here]
        keys = keys * cos_t + pair_swap(keys, 0) * sin_t
        both = jnp.concatenate([keys, kvt[half:, here]], axis=0).astype(BF16)
        for i in range(kv_ref.shape[0]):
            kv_ref[i, tick] = both


def head_rows(score_ref, rewards_ref, group_ref, sample_ref, head_ref):
    rewards = rewards_ref[...]
    samples = rewards.shape[1]
    prompt = lax.broadcasted_iota(jnp.int32, (GROUPS, samples), 0)
    member = prompt == group_ref[...]
    totals = jnp.sum(jnp.where(member, rewards, 0.0), axis=1, keepdims=True)
    own_total = jnp.sum(jnp.where(member, totals, 0.0), axis=0, keepdims=True)
    advantage = rewards - (own_total - rewards) / (GROUP_SIZE - 1)
    sample = lax.broadcasted_iota(jnp.int32, (ROWS, samples), 1)
    row, column = iotas()
    for tick in range(TICKS):
        own = jnp.where(row == column, sample_ref[tick : tick + 1, :].astype(F32), 0.0)
        chosen = sample.astype(F32) == jnp.sum(own, axis=1, keepdims=True)
        row_adv = jnp.sum(jnp.where(chosen, advantage, 0.0), axis=1, keepdims=True)
        head_ref[tick] = (-row_adv * score_ref[tick].astype(F32)).astype(BF16)


def turn_body(grad_ref, out_ref):
    for i in range(out_ref.shape[0]):
        out_ref[i] = grad_ref[...]


def softmaxes(tick, seg_ref, q_ref, keys):
    row, column = iotas()
    allowed = column <= row
    for start in segment_starts(seg_ref, tick):
        allowed = allowed & ((row < start) | (column >= start))
    out = []
    for h in range(q_ref.shape[1] // HD):
        query = q_ref[:, h * HD : (h + 1) * HD]
        weights = jnp.where(allowed, jnp.exp(nn(query, keys) * SCALE), 0.0)
        out.append(weights / jnp.sum(weights, axis=1, keepdims=True))
    return out


def query_body(
    tick,
    odd_ref,
    seg_ref,
    wq_ref,
    gain_ref,
    x_ref,
    kv_ref,
    inv_ref,
    cos_ref,
    sin_ref,
    q_ref,
    soft_ref,
):
    blocks, _, width = x_ref.shape
    shares, half = kv_ref.shape[0], kv_ref.shape[2] // 2
    here = slice(tick * ROWS, (tick + 1) * ROWS)
    query = jnp.zeros(q_ref.shape, F32)
    for j in range(blocks):
        part = slice(j * width, (j + 1) * width)
        xj = x_ref[located(odd_ref, j, shares), here].astype(F32)
        gained = (xj * gain_ref[:, part].astype(F32)).astype(BF16)
        query = query + nn(gained, wq_ref[part, :])
    rotate_heads(query * inv_ref[tick], cos_ref[tick], sin_ref[tick], q_ref)
    keys = jnp.concatenate([kv_ref[i, tick, :half] for i in range(shares)], axis=0)
    for h, softmax in enumerate(softmaxes(tick, seg_ref, q_ref, keys)):
        soft_ref[h] = softmax


def attention_body(
    tick,
    got_at,
    odd_ref,
    seg_ref,
    got_ref,
    wo_ref,
    q_ref,
    kv_ref,
    cos_ref,
    sin_ref,
    *refs,
):
    *ready, dq_ref, dkv_ref, t_ref = refs
    blocks, _, width = got_ref.shape
    shares, half = dkv_ref.shape[0], dkv_ref.shape[1] // 2
    keys = jnp.concatenate([kv_ref[i, tick, :half] for i in range(shares)], axis=0)
    values = jnp.concatenate([kv_ref[i, tick, half:] for i in range(shares)], axis=0)
    cos = cos_ref[tick]
    sin = sin_ref[tick]
    if ready:
        soft = [ready[0][h] for h in range(ready[0].shape[0])]
    else:
        soft = softmaxes(tick, seg_ref, q_ref, keys)
    dout = jnp.zeros(dq_ref.shape, F32)
    for j in range(blocks):
        at = located(odd_ref, j, shares) if tick == 0 else j
        dout = dout + nt(
            got_ref[at, got_at : got_at + ROWS], wo_ref[:, j * width : (j + 1) * width])
    dout = dout.astype(BF16)
    dkeys = jnp.zeros((HD, ROWS), F32)
    dvalues = jnp.zeros((HD, ROWS), F32)
    own = jnp.zeros((ROWS, HD), F32)
    for h in range(dq_ref.shape[1] // HD):
        cols = slice(h * HD, (h + 1) * HD)
        query = q_ref[:, cols]
        dhead = dout[:, cols]
        softmax = soft[h]
        dprobs = nn(dhead, values)
        delta = jnp.sum(softmax * dprobs, axis=1, keepdims=True)
        dscores = (softmax * (dprobs - delta) * SCALE).astype(BF16)
        dquery = nt(dscores, keys)
        dkeys = dkeys + tn(query, dscores)
        dvalues = dvalues + tn(dhead, softmax.astype(BF16))
        own = own + dquery * query.astype(F32)
        dq_ref[:, cols] = (dquery * cos - pair_swap(dquery, 1) * sin).astype(BF16)
    shared = dkeys * keys.astype(F32) + dvalues * values.astype(F32)
    t_ref[...] = jnp.sum(own + shared.T, axis=1, keepdims=True)
    for i in range(shares):
        part = slice(i * half, (i + 1) * half)
        dkv_ref[i, :half] = dkeys[part].astype(BF16)
        dkv_ref[i, half:] = dvalues[part].astype(BF16)


def partial_body(
    tick,
    odd_ref,
    x_ref,
    dq_ref,
    dkv_ref,
    wq_ref,
    wkv_ref,
    gain_ref,
    inv_ref,
    t_ref,
    cost_ref,
    sint_ref,
    out_ref,
):
    blocks, _, width = out_ref.shape
    both = wkv_ref.shape[0]
    half = both // 2
    dkv = dkv_ref[0, :both].astype(F32)
    for i in range(1, dkv_ref.shape[0]):
        dkv = dkv + dkv_ref[i, :both].astype(F32)
    dkeys = dkv[:half]
    dkeys = dkeys * cost_ref[tick] - pair_swap(dkeys, 0) * sint_ref[tick]
    dkv = jnp.concatenate([dkeys, dkv[half:]], axis=0).T.astype(BF16)
    dq = dq_ref[...]
    inverse = inv_ref[tick]
    along = inverse * inverse * t_ref[...] * (1.0 / D)
    for j in range(blocks):
        part = slice(j * width, (j + 1) * width)
        total = nt(dq, wq_ref[part, :]) + nn(dkv, wkv_ref[:, part])
        scaled = total * (inverse * gain_ref[:, part].astype(F32))
        at = located(odd_ref, j, dkv_ref.shape[0])
        xj = x_ref[at, tick * ROWS : (tick + 1) * ROWS].astype(F32)
        out_ref[j] = (scaled - xj * along).astype(BF16)


def ring_down(value, axis):
    count = lax.axis_size(axis)
    return lax.ppermute(value, axis, [(source, (source - 1) % count) for source in range(count)])


def thirds(table):
    parts = []
    for _ in range(3):
        part = table.astype(ml_dtypes.bfloat16)
        parts.append(part)
        table = table - part.astype(np.float32)
    return jnp.asarray(np.stack(parts))


def rotation_tables():
    column = np.arange(HD)
    frequency = np.exp((column // 2).astype(np.float32) * np.float32(-2.0 * math.log(THETA) / HD))
    angles = np.arange(ROWS).astype(np.float32)[:, None] * frequency[None, :].astype(np.float32)
    parity = np.where(column % 2 == 0, -1.0, 1.0).astype(np.float32)
    cos = np.cos(angles).astype(np.float32)
    sin = (np.sin(angles) * parity).astype(np.float32)
    return [thirds(table) for table in (cos, sin, cos.T, sin.T)]


def per_device(
    saved,
    incoming,
    gain,
    w_query,
    w_key,
    w_value,
    w_out,
    seg_lengths,
    score_grad,
    rewards,
    sample_group,
    head_sample,
):
    tp_index = lax.axis_index("tp")
    tp_count = lax.axis_size("tp")
    first_section = lax.axis_index("pipe") == 0
    share = tp_count // KV
    groups = [list(range(g * share, (g + 1) * share)) for g in range(KV)]
    wq, wk, wv, wo = w_query[0], w_key[0].T, w_value[0].T, w_out[0]
    kv_share = wk.shape[0]
    width = saved.shape[3]
    place = (tp_index & (share - 1)).astype(jnp.int32)[None]
    tables = rotation_tables()

    def blocks_of(rows):
        return (jax.ShapeDtypeStruct((tp_count, rows, width), BF16),)

    def exchange(rows):
        return lax.all_to_all(rows, "tp", 0, 0)

    first_flag = first_section.astype(jnp.int32)[None]
    odd = (lax.axis_index("pipe") & 1).astype(jnp.int32)[None]
    saved, place, odd, first_flag, first_section = lax.optimization_barrier(
        (saved, place, odd, first_flag, first_section)
    )
    def stage(blocks, along):
        lines = []
        for section in range(lax.axis_size("pipe")):
            for line in range(share):
                chosen = [
                    line * share + i if (section + along) % 2 == 0 else i * share + line
                    for i in range(share)
                ]
                lines.append([section * tp_count + member for member in chosen])
        return lax.all_to_all(blocks, ("pipe", "tp"), 0, 0, axis_index_groups=lines)

    rows_in = (TICKS + 1) * ROWS
    (spread,) = kernel_call(
        spread_body,
        (jax.ShapeDtypeStruct((share, rows_in, width), BF16),),
        "v",
        (jnp.concatenate([saved[0].reshape(TICKS * ROWS, width), incoming[0]], axis=0),),
    )
    relay, heads = kernel_call(
        relay_body,
        (
            jax.ShapeDtypeStruct((share, share, rows_in, width), BF16),
            jax.ShapeDtypeStruct(score_grad.shape, BF16),
        ),
        "s" + "v" * 5,
        (
            first_flag,
            stage(spread, 0),
            score_grad,
            rewards[None],
            sample_group[None],
            head_sample,
        ),
    )
    first = stage(relay, 1).reshape(tp_count, rows_in, width)

    grad = incoming[0]
    query, kv, inverse, cos, sin, cos_t, sin_t, wkv = kernel_call(
        forward_body,
        (
            jax.ShapeDtypeStruct((ROWS, wq.shape[1]), BF16),
            jax.ShapeDtypeStruct((share, TICKS, 2 * kv_share, ROWS), BF16),
            jax.ShapeDtypeStruct((TICKS, ROWS, 1), F32),
            jax.ShapeDtypeStruct((TICKS, ROWS, HD), F32),
            jax.ShapeDtypeStruct((TICKS, ROWS, HD), F32),
            jax.ShapeDtypeStruct((TICKS, kv_share, ROWS), F32),
            jax.ShapeDtypeStruct((TICKS, kv_share, ROWS), F32),
            jax.ShapeDtypeStruct((2 * kv_share, wk.shape[1]), BF16),
        ),
        "ss" + "v" * 10,
        (place, odd, seg_lengths, wq, wk, wv, gain, *tables, first),
    )
    kv = lax.all_to_all(kv, "tp", 0, 0, axis_index_groups=groups)

    ready = []
    outputs = []
    for tick in range(TICKS):
        if tick == 0:
            got, got_at = first, TICKS * ROWS
        else:
            grad = received
            (packed,) = kernel_call(turn_body, blocks_of(ROWS), "v", (grad,))
            got, got_at = exchange(packed), 0
        dquery, dkv, along = kernel_call(
            functools.partial(attention_body, tick, got_at),
            (
                jax.ShapeDtypeStruct(query.shape, BF16),
                jax.ShapeDtypeStruct((share, 2 * kv_share, ROWS), BF16),
                jax.ShapeDtypeStruct((ROWS, 1), F32),
            ),
            "s" + "v" * (7 + len(ready)),
            (odd, seg_lengths, got, wo, query, kv, cos, sin, *ready),
        )
        dkv = lax.all_to_all(dkv, "tp", 0, 0, axis_index_groups=groups)
        (blocks,) = kernel_call(
            functools.partial(partial_body, tick),
            blocks_of(ROWS),
            "s" + "v" * 10,
            (odd, first, dquery, dkv, wq, wkv, gain, inverse, along, cos_t, sin_t),
        )
        blocks = exchange(blocks)
        if tick == 0:
            blocks, inverse = lax.optimization_barrier((blocks, inverse))
        total = jnp.sum(blocks.astype(F32), axis=0)
        result = (grad.astype(F32) + total).astype(BF16)
        received = ring_down(jnp.where(first_section, heads[tick], result), "pipe")
        if tick == 0:
            later = kernel_call(
                functools.partial(query_body, 1),
                (
                    jax.ShapeDtypeStruct(query.shape, BF16),
                    jax.ShapeDtypeStruct((query.shape[1] // HD, ROWS, ROWS), F32),
                ),
                "s" + "v" * 8,
                (odd, seg_lengths, wq, gain, first, kv, inverse, cos, sin),
            )
            received, result, later = lax.optimization_barrier((received, result, later))
            query, *ready = later
        outputs.append(result)
    return (jnp.stack(outputs, axis=0)[None], received[None])


def solution(mesh):
    placed = (
        P("pipe", None, None, "tp"),
        P("pipe", None, "tp"),
        P("pipe", None),
        P("pipe", None, "tp"),
        P("pipe", None, "tp"),
        P("pipe", None, "tp"),
        P("pipe", "tp", None),
        P("pipe", None, None),
        P(None, None, "tp"),
        P(),
        P(),
        P(),
    )
    return jax.shard_map(
        per_device,
        mesh=mesh,
        in_specs=placed,
        out_specs=(P("pipe", None, None, "tp"), P("pipe", None, "tp")),
        check_vma=False,
    )
```

```python
import functools
import math

import jax
import jax.numpy as jnp
import ml_dtypes
import numpy as np
from jax import lax
from jax.experimental import pallas as pl
from jax.experimental.pallas import tpu as pltpu
from jax.sharding import PartitionSpec as P

D = 4096
KV = 4
HD = 128
ROWS = 128
TICKS = 2
GROUP_SIZE = 16
GROUPS = 32

EPS = 1e-05
THETA = 500000.0
SCALE = 1.0 / math.sqrt(HD)
F32 = jnp.float32
BF16 = jnp.bfloat16
VMEM_LIMIT = 16 * 1024 * 1024


def nn(a, b):
    return lax.dot_general(a, b, (((1,), (0,)), ((), ())), preferred_element_type=F32)


def nt(a, b):
    return lax.dot_general(a, b, (((1,), (1,)), ((), ())), preferred_element_type=F32)


def tn(a, b):
    return lax.dot_general(a, b, (((0,), (0,)), ((), ())), preferred_element_type=F32)


def pair_swap(v, axis):
    n = v.shape[axis]
    even = lax.broadcasted_iota(jnp.int32, v.shape, axis) % 2 == 0
    return jnp.where(even, pltpu.roll(v, n - 1, axis), pltpu.roll(v, 1, axis))


def kernel_call(body, outs, specs, args):
    vmem = pl.BlockSpec(memory_space=pltpu.VMEM)
    kinds = {
        "v": vmem,
        "s": pl.BlockSpec(memory_space=pltpu.SMEM),
    }
    return pl.pallas_call(
        body,
        out_shape=outs,
        in_specs=[kinds[kind] for kind in specs],
        out_specs=[vmem] * len(outs),
        compiler_params=pltpu.CompilerParams(vmem_limit_bytes=VMEM_LIMIT),
    )(*args)


def segment_starts(seg_ref, tick):
    lengths = seg_ref[0, tick : tick + 1, :].astype(F32)
    index = lax.broadcasted_iota(jnp.int32, lengths.shape, 1)
    return [
        jnp.sum(jnp.where(index < g, lengths, 0.0), axis=1, keepdims=True)
        for g in range(1, lengths.shape[1])
    ]


def iotas():
    row = lax.broadcasted_iota(jnp.int32, (ROWS, ROWS), 0).astype(F32)
    column = lax.broadcasted_iota(jnp.int32, (ROWS, ROWS), 1).astype(F32)
    return row, column


def position_match(seg_ref, tick):
    row, column = iotas()
    begin = jnp.zeros(row.shape, F32)
    for start in segment_starts(seg_ref, tick):
        begin = jnp.where(row >= start, start, begin)
    return jnp.where(column == row - begin, 1.0, 0.0).astype(BF16)


def located(odd_ref, block, share):
    across = block % share * share + block // share
    return jnp.where(odd_ref[0] > 0, across, block)


def relay_body(
    first_ref, got_ref, score_ref, rewards_ref, group_ref, sample_ref, out_ref, head_ref
):
    @pl.when(first_ref[0] > 0)
    def _():
        head_rows(score_ref, rewards_ref, group_ref, sample_ref, head_ref)

    for i in range(out_ref.shape[0]):
        out_ref[i] = got_ref[...]


def spread_body(rows_ref, out_ref):
    for i in range(out_ref.shape[0]):
        out_ref[i] = rows_ref[...]


def row_tables(match, ctab_ref, stab_ref):
    cos = sum(nn(match, ctab_ref[i]) for i in range(3))
    sin = sum(nn(match, stab_ref[i]) for i in range(3))
    return cos, sin


def rotate_heads(query, cos, sin, q_ref):
    for h in range(query.shape[1] // HD):
        cols = slice(h * HD, (h + 1) * HD)
        head = query[:, cols]
        q_ref[:, cols] = (head * cos + pair_swap(head, 1) * sin).astype(BF16)


def forward_body(
    place_ref,
    odd_ref,
    seg_ref,
    wq_ref,
    wk_ref,
    wv_ref,
    gain_ref,
    ctab_ref,
    stab_ref,
    ctabt_ref,
    stabt_ref,
    x_ref,
    q_ref,
    kv_ref,
    inv_ref,
    cos_ref,
    sin_ref,
    cost_ref,
    sint_ref,
    wkv_ref,
):
    half = wk_ref.shape[0]
    wkv_ref[:half] = wk_ref[...]
    wkv_ref[half:] = wv_ref[...]
    blocks, _, width = x_ref.shape
    rows = TICKS * ROWS
    q_rows = ROWS
    own = pl.ds(pl.multiple_of(place_ref[0] * half, half), half)
    squares = jnp.zeros((rows, width), F32)
    query = jnp.zeros((q_rows, wq_ref.shape[1]), F32)
    kvt = jnp.zeros((2 * half, rows), F32)
    for j in range(blocks):
        part = slice(j * width, (j + 1) * width)
        xj = x_ref[located(odd_ref, j, kv_ref.shape[0]), :rows].astype(F32)
        squares = squares + xj * xj
        gained = (xj * gain_ref[:, part].astype(F32)).astype(BF16)
        query = query + nn(gained[:q_rows], wq_ref[part, :])
        kvt = kvt + nt(wkv_ref[:, part], gained)
    inverse = lax.rsqrt(jnp.sum(squares, axis=1, keepdims=True) * (1.0 / D) + EPS)
    eye = lax.broadcasted_iota(jnp.int32, (rows, rows), 0) == lax.broadcasted_iota(
        jnp.int32, (rows, rows), 1
    )
    kvt = kvt * jnp.sum(jnp.where(eye, inverse, 0.0), axis=0, keepdims=True)
    query = query * inverse[:q_rows]
    for tick in range(TICKS):
        here = slice(tick * ROWS, (tick + 1) * ROWS)
        inv_ref[tick] = inverse[here]
        match = position_match(seg_ref, tick)
        cos_t = sum(nt(ctabt_ref[i, own, :], match) for i in range(3))
        sin_t = sum(nt(stabt_ref[i, own, :], match) for i in range(3))
        cost_ref[tick] = cos_t
        sint_ref[tick] = sin_t
        if tick == 0:
            cos, sin = row_tables(match, ctab_ref, stab_ref)
            cos_ref[...] = cos
            sin_ref[...] = sin
            rotate_heads(query, cos, sin, q_ref)
        keys = kvt[:half, here]
        keys = keys * cos_t + pair_swap(keys, 0) * sin_t
        both = jnp.concatenate([keys, kvt[half:, here]], axis=0).astype(BF16)
        for i in range(kv_ref.shape[0]):
            kv_ref[i, tick] = both


def head_rows(score_ref, rewards_ref, group_ref, sample_ref, head_ref):
    rewards = rewards_ref[...]
    samples = rewards.shape[1]
    prompt = lax.broadcasted_iota(jnp.int32, (GROUPS, samples), 0)
    member = prompt == group_ref[...]
    totals = jnp.sum(jnp.where(member, rewards, 0.0), axis=1, keepdims=True)
    own_total = jnp.sum(jnp.where(member, totals, 0.0), axis=0, keepdims=True)
    advantage = rewards - (own_total - rewards) / (GROUP_SIZE - 1)
    sample = lax.broadcasted_iota(jnp.int32, (ROWS, samples), 1)
    row, column = iotas()
    for tick in range(TICKS):
        own = jnp.where(row == column, sample_ref[tick : tick + 1, :].astype(F32), 0.0)
        chosen = sample.astype(F32) == jnp.sum(own, axis=1, keepdims=True)
        row_adv = jnp.sum(jnp.where(chosen, advantage, 0.0), axis=1, keepdims=True)
        head_ref[tick] = (-row_adv * score_ref[tick].astype(F32)).astype(BF16)


def turn_body(grad_ref, out_ref):
    for i in range(out_ref.shape[0]):
        out_ref[i] = grad_ref[...]


def softmaxes(tick, seg_ref, q_ref, keys):
    row, column = iotas()
    allowed = column <= row
    for start in segment_starts(seg_ref, tick):
        allowed = allowed & ((row < start) | (column >= start))
    out = []
    for h in range(q_ref.shape[1] // HD):
        query = q_ref[:, h * HD : (h + 1) * HD]
        weights = jnp.where(allowed, jnp.exp(nn(query, keys) * SCALE), 0.0)
        out.append(weights * (1.0 / jnp.sum(weights, axis=1, keepdims=True)))
    return out


def query_body(
    tick,
    odd_ref,
    seg_ref,
    wq_ref,
    gain_ref,
    x_ref,
    kv_ref,
    inv_ref,
    ctab_ref,
    stab_ref,
    q_ref,
    soft_ref,
    cos_ref,
    sin_ref,
):
    blocks, _, width = x_ref.shape
    shares, half = kv_ref.shape[0], kv_ref.shape[2] // 2
    here = slice(tick * ROWS, (tick + 1) * ROWS)
    query = jnp.zeros(q_ref.shape, F32)
    for j in range(blocks):
        part = slice(j * width, (j + 1) * width)
        xj = x_ref[located(odd_ref, j, shares), here].astype(F32)
        gained = (xj * gain_ref[:, part].astype(F32)).astype(BF16)
        query = query + nn(gained, wq_ref[part, :])
    cos, sin = row_tables(position_match(seg_ref, tick), ctab_ref, stab_ref)
    cos_ref[...] = cos
    sin_ref[...] = sin
    rotate_heads(query * inv_ref[tick], cos, sin, q_ref)
    keys = jnp.concatenate([kv_ref[i, tick, :half] for i in range(shares)], axis=0)
    for h, softmax in enumerate(softmaxes(tick, seg_ref, q_ref, keys)):
        soft_ref[h] = softmax


def attention_body(
    tick,
    got_at,
    odd_ref,
    seg_ref,
    got_ref,
    wo_ref,
    q_ref,
    kv_ref,
    cos_ref,
    sin_ref,
    *refs,
):
    *ready, dq_ref, dkv_ref, t_ref = refs
    blocks, _, width = got_ref.shape
    shares, half = dkv_ref.shape[0], dkv_ref.shape[1] // 2
    keys = jnp.concatenate([kv_ref[i, tick, :half] for i in range(shares)], axis=0)
    values = jnp.concatenate([kv_ref[i, tick, half:] for i in range(shares)], axis=0)
    cos = cos_ref[...]
    sin = sin_ref[...]
    if ready:
        soft = [ready[0][h] for h in range(ready[0].shape[0])]
    else:
        soft = softmaxes(tick, seg_ref, q_ref, keys)
    dout = jnp.zeros(dq_ref.shape, F32)
    for j in range(blocks):
        at = located(odd_ref, j, shares) if tick == 0 else j
        dout = dout + nt(
            got_ref[at, got_at : got_at + ROWS], wo_ref[:, j * width : (j + 1) * width])
    dout = dout.astype(BF16)
    dkeys = jnp.zeros((HD, ROWS), F32)
    dvalues = jnp.zeros((HD, ROWS), F32)
    own = jnp.zeros((ROWS, HD), F32)
    for h in range(dq_ref.shape[1] // HD):
        cols = slice(h * HD, (h + 1) * HD)
        query = q_ref[:, cols]
        dhead = dout[:, cols]
        softmax = soft[h]
        dprobs = nn(dhead, values)
        delta = jnp.sum(softmax * dprobs, axis=1, keepdims=True)
        dscores = (softmax * (dprobs - delta) * SCALE).astype(BF16)
        dquery = nt(dscores, keys)
        dkeys = dkeys + tn(query, dscores)
        dvalues = dvalues + tn(dhead, softmax.astype(BF16))
        own = own + dquery * query.astype(F32)
        dq_ref[:, cols] = (dquery * cos - pair_swap(dquery, 1) * sin).astype(BF16)
    shared = dkeys * keys.astype(F32) + dvalues * values.astype(F32)
    shared = jnp.sum(shared, axis=0, keepdims=True)
    row, column = iotas()
    t_ref[...] = jnp.sum(own + jnp.where(row == column, shared, 0.0), axis=1, keepdims=True)
    for i in range(shares):
        part = slice(i * half, (i + 1) * half)
        dkv_ref[i, :half] = dkeys[part].astype(BF16)
        dkv_ref[i, half:] = dvalues[part].astype(BF16)


def partial_body(
    tick,
    odd_ref,
    x_ref,
    dq_ref,
    dkv_ref,
    wq_ref,
    wkv_ref,
    gain_ref,
    inv_ref,
    t_ref,
    cost_ref,
    sint_ref,
    out_ref,
):
    blocks, _, width = out_ref.shape
    both = wkv_ref.shape[0]
    half = both // 2
    dkv = dkv_ref[0, :both].astype(F32)
    for i in range(1, dkv_ref.shape[0]):
        dkv = dkv + dkv_ref[i, :both].astype(F32)
    dkeys = dkv[:half]
    dkeys = dkeys * cost_ref[tick] - pair_swap(dkeys, 0) * sint_ref[tick]
    dkv = jnp.concatenate([dkeys, dkv[half:]], axis=0).T.astype(BF16)
    dq = dq_ref[...]
    inverse = inv_ref[tick]
    along = inverse * inverse * t_ref[...] * (1.0 / D)
    for j in range(blocks):
        part = slice(j * width, (j + 1) * width)
        total = nt(dq, wq_ref[part, :]) + nn(dkv, wkv_ref[:, part])
        scaled = total * (inverse * gain_ref[:, part].astype(F32))
        at = located(odd_ref, j, dkv_ref.shape[0])
        xj = x_ref[at, tick * ROWS : (tick + 1) * ROWS].astype(F32)
        out_ref[j] = (scaled - xj * along).astype(BF16)


def ring_down(value, axis):
    count = lax.axis_size(axis)
    return lax.ppermute(value, axis, [(source, (source - 1) % count) for source in range(count)])


def thirds(table):
    parts = []
    for _ in range(3):
        part = table.astype(ml_dtypes.bfloat16)
        parts.append(part)
        table = table - part.astype(np.float32)
    return jnp.asarray(np.stack(parts))


def rotation_tables():
    column = np.arange(HD)
    frequency = np.exp((column // 2).astype(np.float32) * np.float32(-2.0 * math.log(THETA) / HD))
    angles = np.arange(ROWS).astype(np.float32)[:, None] * frequency[None, :].astype(np.float32)
    parity = np.where(column % 2 == 0, -1.0, 1.0).astype(np.float32)
    cos = np.cos(angles).astype(np.float32)
    sin = (np.sin(angles) * parity).astype(np.float32)
    return [thirds(table) for table in (cos, sin, cos.T, sin.T)]


def per_device(
    saved,
    incoming,
    gain,
    w_query,
    w_key,
    w_value,
    w_out,
    seg_lengths,
    score_grad,
    rewards,
    sample_group,
    head_sample,
):
    tp_index = lax.axis_index("tp")
    tp_count = lax.axis_size("tp")
    first_section = lax.axis_index("pipe") == 0
    share = tp_count // KV
    groups = [list(range(g * share, (g + 1) * share)) for g in range(KV)]
    wq, wk, wv, wo = w_query[0], w_key[0].T, w_value[0].T, w_out[0]
    kv_share = wk.shape[0]
    width = saved.shape[3]
    place = (tp_index & (share - 1)).astype(jnp.int32)[None]
    tables = rotation_tables()

    def blocks_of(rows):
        return (jax.ShapeDtypeStruct((tp_count, rows, width), BF16),)

    def exchange(rows):
        return lax.all_to_all(rows, "tp", 0, 0)

    first_flag = first_section.astype(jnp.int32)[None]
    odd = (lax.axis_index("pipe") & 1).astype(jnp.int32)[None]
    saved, place, odd, first_flag, first_section = lax.optimization_barrier(
        (saved, place, odd, first_flag, first_section)
    )
    def stage(blocks, along):
        lines = []
        for section in range(lax.axis_size("pipe")):
            for line in range(share):
                chosen = [
                    line * share + i if (section + along) % 2 == 0 else i * share + line
                    for i in range(share)
                ]
                lines.append([section * tp_count + member for member in chosen])
        return lax.all_to_all(blocks, ("pipe", "tp"), 0, 0, axis_index_groups=lines)

    rows_in = (TICKS + 1) * ROWS
    (spread,) = kernel_call(
        spread_body,
        (jax.ShapeDtypeStruct((share, rows_in, width), BF16),),
        "v",
        (jnp.concatenate([saved[0].reshape(TICKS * ROWS, width), incoming[0]], axis=0),),
    )
    relay, heads = kernel_call(
        relay_body,
        (
            jax.ShapeDtypeStruct((share, share, rows_in, width), BF16),
            jax.ShapeDtypeStruct(score_grad.shape, BF16),
        ),
        "s" + "v" * 5,
        (
            first_flag,
            stage(spread, 0),
            score_grad,
            rewards[None],
            sample_group[None],
            head_sample,
        ),
    )
    first = stage(relay, 1).reshape(tp_count, rows_in, width)

    grad = incoming[0]
    query, kv, inverse, cos, sin, cos_t, sin_t, wkv = kernel_call(
        forward_body,
        (
            jax.ShapeDtypeStruct((ROWS, wq.shape[1]), BF16),
            jax.ShapeDtypeStruct((share, TICKS, 2 * kv_share, ROWS), BF16),
            jax.ShapeDtypeStruct((TICKS, ROWS, 1), F32),
            jax.ShapeDtypeStruct((ROWS, HD), F32),
            jax.ShapeDtypeStruct((ROWS, HD), F32),
            jax.ShapeDtypeStruct((TICKS, kv_share, ROWS), F32),
            jax.ShapeDtypeStruct((TICKS, kv_share, ROWS), F32),
            jax.ShapeDtypeStruct((2 * kv_share, wk.shape[1]), BF16),
        ),
        "ss" + "v" * 10,
        (place, odd, seg_lengths, wq, wk, wv, gain, *tables, first),
    )
    kv = lax.all_to_all(kv, "tp", 0, 0, axis_index_groups=groups)

    ready = []
    outputs = []
    for tick in range(TICKS):
        if tick == 0:
            got, got_at = first, TICKS * ROWS
        else:
            grad = received
            (packed,) = kernel_call(turn_body, blocks_of(ROWS), "v", (grad,))
            got, got_at = exchange(packed), 0
        dquery, dkv, along = kernel_call(
            functools.partial(attention_body, tick, got_at),
            (
                jax.ShapeDtypeStruct(query.shape, BF16),
                jax.ShapeDtypeStruct((share, 2 * kv_share, ROWS), BF16),
                jax.ShapeDtypeStruct((ROWS, 1), F32),
            ),
            "s" + "v" * (7 + len(ready)),
            (odd, seg_lengths, got, wo, query, kv, cos, sin, *ready),
        )
        dkv = lax.all_to_all(dkv, "tp", 0, 0, axis_index_groups=groups)
        (blocks,) = kernel_call(
            functools.partial(partial_body, tick),
            blocks_of(ROWS),
            "s" + "v" * 10,
            (odd, first, dquery, dkv, wq, wkv, gain, inverse, along, cos_t, sin_t),
        )
        blocks = exchange(blocks)
        if tick == 0:
            blocks, inverse = lax.optimization_barrier((blocks, inverse))
        total = jnp.sum(blocks.astype(F32), axis=0)
        result = (grad.astype(F32) + total).astype(BF16)
        received = ring_down(jnp.where(first_section, heads[tick], result), "pipe")
        if tick == 0:
            later = kernel_call(
                functools.partial(query_body, 1),
                (
                    jax.ShapeDtypeStruct(query.shape, BF16),
                    jax.ShapeDtypeStruct((query.shape[1] // HD, ROWS, ROWS), F32),
                    jax.ShapeDtypeStruct((ROWS, HD), F32),
                    jax.ShapeDtypeStruct((ROWS, HD), F32),
                ),
                "s" + "v" * 8,
                (odd, seg_lengths, wq, gain, first, kv, inverse, tables[0], tables[1]),
            )
            received, result, later = lax.optimization_barrier((received, result, later))
            query, *ready, cos, sin = later
        outputs.append(result)
    return (jnp.stack(outputs, axis=0)[None], received[None])


def solution(mesh):
    placed = (
        P("pipe", None, None, "tp"),
        P("pipe", None, "tp"),
        P("pipe", None),
        P("pipe", None, "tp"),
        P("pipe", None, "tp"),
        P("pipe", None, "tp"),
        P("pipe", "tp", None),
        P("pipe", None, None),
        P(None, None, "tp"),
        P(),
        P(),
        P(),
    )
    return jax.shard_map(
        per_device,
        mesh=mesh,
        in_specs=placed,
        out_specs=(P("pipe", None, None, "tp"), P("pipe", None, "tp")),
        check_vma=False,
    )
```

```python
import functools
import math

import jax
import jax.numpy as jnp
import ml_dtypes
import numpy as np
from jax import lax
from jax.experimental import pallas as pl
from jax.experimental.pallas import tpu as pltpu
from jax.sharding import PartitionSpec as P

D = 4096
KV = 4
HD = 128
ROWS = 128
TICKS = 2
GROUP_SIZE = 16
GROUPS = 32

EPS = 1e-05
THETA = 500000.0
SCALE = 1.0 / math.sqrt(HD)
F32 = jnp.float32
BF16 = jnp.bfloat16
VMEM_LIMIT = 16 * 1024 * 1024


def nn(a, b):
    return lax.dot_general(a, b, (((1,), (0,)), ((), ())), preferred_element_type=F32)


def nt(a, b):
    return lax.dot_general(a, b, (((1,), (1,)), ((), ())), preferred_element_type=F32)


def tn(a, b):
    return lax.dot_general(a, b, (((0,), (0,)), ((), ())), preferred_element_type=F32)


def pair_swap(v, axis):
    n = v.shape[axis]
    even = lax.broadcasted_iota(jnp.int32, v.shape, axis) % 2 == 0
    return jnp.where(even, pltpu.roll(v, n - 1, axis), pltpu.roll(v, 1, axis))


def kernel_call(body, outs, specs, args):
    vmem = pl.BlockSpec(memory_space=pltpu.VMEM)
    kinds = {
        "v": vmem,
        "s": pl.BlockSpec(memory_space=pltpu.SMEM),
    }
    return pl.pallas_call(
        body,
        out_shape=outs,
        in_specs=[kinds[kind] for kind in specs],
        out_specs=[vmem] * len(outs),
        compiler_params=pltpu.CompilerParams(vmem_limit_bytes=VMEM_LIMIT),
    )(*args)


def segment_starts(seg_ref, tick):
    lengths = seg_ref[0, tick : tick + 1, :].astype(F32)
    index = lax.broadcasted_iota(jnp.int32, lengths.shape, 1)
    return [
        jnp.sum(jnp.where(index < g, lengths, 0.0), axis=1, keepdims=True)
        for g in range(1, lengths.shape[1])
    ]


def iotas():
    row = lax.broadcasted_iota(jnp.int32, (ROWS, ROWS), 0).astype(F32)
    column = lax.broadcasted_iota(jnp.int32, (ROWS, ROWS), 1).astype(F32)
    return row, column


def position_match(seg_ref, tick):
    row, column = iotas()
    begin = jnp.zeros(row.shape, F32)
    for start in segment_starts(seg_ref, tick):
        begin = jnp.where(row >= start, start, begin)
    return jnp.where(column == row - begin, 1.0, 0.0).astype(BF16)


def located(odd_ref, block, share):
    across = block % share * share + block // share
    return jnp.where(odd_ref[0] > 0, across, block)


def relay_body(
    first_ref, got_ref, score_ref, rewards_ref, group_ref, sample_ref, out_ref, head_ref
):
    @pl.when(first_ref[0] > 0)
    def _():
        head_rows(score_ref, rewards_ref, group_ref, sample_ref, head_ref)

    for i in range(out_ref.shape[0]):
        out_ref[i] = got_ref[...]


def spread_body(rows_ref, out_ref):
    for i in range(out_ref.shape[0]):
        out_ref[i] = rows_ref[...]


def row_tables(match, ctab_ref, stab_ref):
    cos = sum(nn(match, ctab_ref[i]) for i in range(3))
    sin = sum(nn(match, stab_ref[i]) for i in range(3))
    return cos, sin


def rotate_heads(query, cos, sin, q_ref):
    for h in range(query.shape[1] // HD):
        cols = slice(h * HD, (h + 1) * HD)
        head = query[:, cols]
        q_ref[:, cols] = (head * cos + pair_swap(head, 1) * sin).astype(BF16)


def forward_body(
    place_ref,
    odd_ref,
    seg_ref,
    wq_ref,
    wk_ref,
    wv_ref,
    gain_ref,
    ctab_ref,
    stab_ref,
    ctabt_ref,
    stabt_ref,
    x_ref,
    q_ref,
    kv_ref,
    inv_ref,
    cos_ref,
    sin_ref,
    cost_ref,
    sint_ref,
    wkv_ref,
):
    half = wk_ref.shape[0]
    wkv_ref[:half] = wk_ref[...]
    wkv_ref[half:] = wv_ref[...]
    blocks, _, width = x_ref.shape
    rows = TICKS * ROWS
    q_rows = ROWS
    own = pl.ds(pl.multiple_of(place_ref[0] * half, half), half)
    squares = jnp.zeros((rows, width), F32)
    query = jnp.zeros((q_rows, wq_ref.shape[1]), F32)
    kvt = jnp.zeros((2 * half, rows), F32)
    for j in range(blocks):
        part = slice(j * width, (j + 1) * width)
        xj = x_ref[located(odd_ref, j, kv_ref.shape[0]), :rows].astype(F32)
        squares = squares + xj * xj
        gained = (xj * gain_ref[:, part].astype(F32)).astype(BF16)
        query = query + nn(gained[:q_rows], wq_ref[part, :])
        kvt = kvt + nt(wkv_ref[:, part], gained)
    inverse = lax.rsqrt(jnp.sum(squares, axis=1, keepdims=True) * (1.0 / D) + EPS)
    eye = lax.broadcasted_iota(jnp.int32, (rows, rows), 0) == lax.broadcasted_iota(
        jnp.int32, (rows, rows), 1
    )
    kvt = kvt * jnp.sum(jnp.where(eye, inverse, 0.0), axis=0, keepdims=True)
    query = query * inverse[:q_rows]
    for tick in range(TICKS):
        here = slice(tick * ROWS, (tick + 1) * ROWS)
        inv_ref[tick] = inverse[here]
        match = position_match(seg_ref, tick)
        cos_t = sum(nt(ctabt_ref[i, own, :], match) for i in range(3))
        sin_t = sum(nt(stabt_ref[i, own, :], match) for i in range(3))
        cost_ref[tick] = cos_t
        sint_ref[tick] = sin_t
        if tick == 0:
            cos, sin = row_tables(match, ctab_ref, stab_ref)
            cos_ref[...] = cos
            sin_ref[...] = sin
            rotate_heads(query, cos, sin, q_ref)
        keys = kvt[:half, here]
        keys = keys * cos_t + pair_swap(keys, 0) * sin_t
        both = jnp.concatenate([keys, kvt[half:, here]], axis=0).astype(BF16)
        for i in range(kv_ref.shape[0]):
            kv_ref[i, tick] = both


def head_rows(score_ref, rewards_ref, group_ref, sample_ref, head_ref):
    rewards = rewards_ref[...]
    samples = rewards.shape[1]
    prompt = lax.broadcasted_iota(jnp.int32, (GROUPS, samples), 0)
    member = prompt == group_ref[...]
    totals = jnp.sum(jnp.where(member, rewards, 0.0), axis=1, keepdims=True)
    own_total = jnp.sum(jnp.where(member, totals, 0.0), axis=0, keepdims=True)
    advantage = rewards - (own_total - rewards) / (GROUP_SIZE - 1)
    sample = lax.broadcasted_iota(jnp.int32, (ROWS, samples), 1)
    row, column = iotas()
    for tick in range(TICKS):
        own = jnp.where(row == column, sample_ref[tick : tick + 1, :].astype(F32), 0.0)
        chosen = sample.astype(F32) == jnp.sum(own, axis=1, keepdims=True)
        row_adv = jnp.sum(jnp.where(chosen, advantage, 0.0), axis=1, keepdims=True)
        head_ref[tick] = (-row_adv * score_ref[tick].astype(F32)).astype(BF16)


def turn_body(grad_ref, out_ref):
    for i in range(out_ref.shape[0]):
        out_ref[i] = grad_ref[...]


def softmaxes(tick, seg_ref, q_ref, keys):
    row, column = iotas()
    allowed = column <= row
    for start in segment_starts(seg_ref, tick):
        allowed = allowed & ((row < start) | (column >= start))
    out = []
    for h in range(q_ref.shape[1] // HD):
        query = q_ref[:, h * HD : (h + 1) * HD]
        weights = jnp.where(allowed, jnp.exp(nn(query, keys) * SCALE), 0.0)
        out.append(weights * (1.0 / jnp.sum(weights, axis=1, keepdims=True)))
    return out


def query_body(
    tick,
    odd_ref,
    seg_ref,
    wq_ref,
    gain_ref,
    x_ref,
    kv_ref,
    inv_ref,
    ctab_ref,
    stab_ref,
    q_ref,
    soft_ref,
    cos_ref,
    sin_ref,
):
    blocks, _, width = x_ref.shape
    shares, half = kv_ref.shape[0], kv_ref.shape[2] // 2
    here = slice(tick * ROWS, (tick + 1) * ROWS)
    query = jnp.zeros(q_ref.shape, F32)
    for j in range(blocks):
        part = slice(j * width, (j + 1) * width)
        xj = x_ref[located(odd_ref, j, shares), here].astype(F32)
        gained = (xj * gain_ref[:, part].astype(F32)).astype(BF16)
        query = query + nn(gained, wq_ref[part, :])
    cos, sin = row_tables(position_match(seg_ref, tick), ctab_ref, stab_ref)
    cos_ref[...] = cos
    sin_ref[...] = sin
    rotate_heads(query * inv_ref[tick], cos, sin, q_ref)
    keys = jnp.concatenate([kv_ref[i, tick, :half] for i in range(shares)], axis=0)
    for h, softmax in enumerate(softmaxes(tick, seg_ref, q_ref, keys)):
        soft_ref[h] = softmax


def attention_body(
    tick,
    got_at,
    odd_ref,
    seg_ref,
    got_ref,
    wo_ref,
    q_ref,
    kv_ref,
    cos_ref,
    sin_ref,
    *refs,
):
    *ready, dq_ref, dkv_ref, t_ref = refs
    blocks, _, width = got_ref.shape
    shares, half = dkv_ref.shape[0], dkv_ref.shape[1] // 2
    keys = jnp.concatenate([kv_ref[i, tick, :half] for i in range(shares)], axis=0)
    values = jnp.concatenate([kv_ref[i, tick, half:] for i in range(shares)], axis=0)
    cos = cos_ref[...]
    sin = sin_ref[...]
    if ready:
        soft = [ready[0][h] for h in range(ready[0].shape[0])]
    else:
        soft = softmaxes(tick, seg_ref, q_ref, keys)
    dout = jnp.zeros(dq_ref.shape, F32)
    for j in range(blocks):
        at = located(odd_ref, j, shares) if tick == 0 else j
        dout = dout + nt(
            got_ref[at, got_at : got_at + ROWS], wo_ref[:, j * width : (j + 1) * width])
    dout = dout.astype(BF16)
    dkeys = jnp.zeros((HD, ROWS), F32)
    dvalues = jnp.zeros((HD, ROWS), F32)
    own = jnp.zeros((ROWS, HD), F32)
    for h in range(dq_ref.shape[1] // HD):
        cols = slice(h * HD, (h + 1) * HD)
        query = q_ref[:, cols]
        dhead = dout[:, cols]
        softmax = soft[h]
        dprobs = nn(dhead, values)
        delta = jnp.sum(softmax * dprobs, axis=1, keepdims=True)
        dscores = (softmax * (dprobs - delta) * SCALE).astype(BF16)
        dquery = nt(dscores, keys)
        dkeys = dkeys + tn(query, dscores)
        dvalues = dvalues + tn(dhead, softmax.astype(BF16))
        own = own + dquery * query.astype(F32)
        dq_ref[:, cols] = (dquery * cos - pair_swap(dquery, 1) * sin).astype(BF16)
    shared = dkeys * keys.astype(F32) + dvalues * values.astype(F32)
    shared = jnp.sum(shared, axis=0, keepdims=True)
    row, column = iotas()
    t_ref[...] = jnp.sum(own + jnp.where(row == column, shared, 0.0), axis=1, keepdims=True)
    for i in range(shares):
        part = slice(i * half, (i + 1) * half)
        dkv_ref[i, :half] = dkeys[part].astype(BF16)
        dkv_ref[i, half:] = dvalues[part].astype(BF16)


def partial_body(
    tick,
    odd_ref,
    x_ref,
    dq_ref,
    dkv_ref,
    wq_ref,
    wkv_ref,
    gain_ref,
    inv_ref,
    t_ref,
    cost_ref,
    sint_ref,
    out_ref,
):
    blocks, _, width = out_ref.shape
    both = wkv_ref.shape[0]
    half = both // 2
    dkv = dkv_ref[0, :both].astype(F32)
    for i in range(1, dkv_ref.shape[0]):
        dkv = dkv + dkv_ref[i, :both].astype(F32)
    dkeys = dkv[:half]
    dkeys = dkeys * cost_ref[tick] - pair_swap(dkeys, 0) * sint_ref[tick]
    dkv = jnp.concatenate([dkeys, dkv[half:]], axis=0).T.astype(BF16)
    dq = dq_ref[...]
    inverse = inv_ref[tick]
    along = inverse * inverse * t_ref[...] * (1.0 / D)
    for j in range(blocks):
        part = slice(j * width, (j + 1) * width)
        total = nt(dq, wq_ref[part, :]) + nn(dkv, wkv_ref[:, part])
        scaled = total * (inverse * gain_ref[:, part].astype(F32))
        at = located(odd_ref, j, dkv_ref.shape[0])
        xj = x_ref[at, tick * ROWS : (tick + 1) * ROWS].astype(F32)
        out_ref[j] = (scaled - xj * along).astype(BF16)


def ring_down(value, axis):
    count = lax.axis_size(axis)
    return lax.ppermute(value, axis, [(source, (source - 1) % count) for source in range(count)])


def thirds(table):
    parts = []
    for _ in range(3):
        part = table.astype(ml_dtypes.bfloat16)
        parts.append(part)
        table = table - part.astype(np.float32)
    return jnp.asarray(np.stack(parts))


def rotation_tables():
    column = np.arange(HD)
    frequency = np.exp((column // 2).astype(np.float32) * np.float32(-2.0 * math.log(THETA) / HD))
    angles = np.arange(ROWS).astype(np.float32)[:, None] * frequency[None, :].astype(np.float32)
    parity = np.where(column % 2 == 0, -1.0, 1.0).astype(np.float32)
    cos = np.cos(angles).astype(np.float32)
    sin = (np.sin(angles) * parity).astype(np.float32)
    return [thirds(table) for table in (cos, sin, cos.T, sin.T)]


def per_device(
    saved,
    incoming,
    gain,
    w_query,
    w_key,
    w_value,
    w_out,
    seg_lengths,
    score_grad,
    rewards,
    sample_group,
    head_sample,
):
    tp_index = lax.axis_index("tp")
    tp_count = lax.axis_size("tp")
    first_section = lax.axis_index("pipe") == 0
    share = tp_count // KV
    groups = [list(range(g * share, (g + 1) * share)) for g in range(KV)]
    wq, wk, wv, wo = w_query[0], w_key[0].T, w_value[0].T, w_out[0]
    kv_share = wk.shape[0]
    width = saved.shape[3]
    place = (tp_index & (share - 1)).astype(jnp.int32)[None]
    tables = rotation_tables()

    def blocks_of(rows):
        return (jax.ShapeDtypeStruct((tp_count, rows, width), BF16),)

    def exchange(rows):
        return lax.all_to_all(rows, "tp", 0, 0)

    first_flag = first_section.astype(jnp.int32)[None]
    odd = (1 - (lax.axis_index("pipe") & 1)).astype(jnp.int32)[None]
    saved, place, odd, first_flag, first_section = lax.optimization_barrier(
        (saved, place, odd, first_flag, first_section)
    )
    def stage(blocks, along):
        lines = []
        for section in range(lax.axis_size("pipe")):
            for line in range(share):
                chosen = [
                    line * share + i if (section + along) % 2 == 1 else i * share + line
                    for i in range(share)
                ]
                lines.append([section * tp_count + member for member in chosen])
        return lax.all_to_all(blocks, ("pipe", "tp"), 0, 0, axis_index_groups=lines)

    rows_in = (TICKS + 1) * ROWS
    (spread,) = kernel_call(
        spread_body,
        (jax.ShapeDtypeStruct((share, rows_in, width), BF16),),
        "v",
        (jnp.concatenate([saved[0].reshape(TICKS * ROWS, width), incoming[0]], axis=0),),
    )
    relay, heads = kernel_call(
        relay_body,
        (
            jax.ShapeDtypeStruct((share, share, rows_in, width), BF16),
            jax.ShapeDtypeStruct(score_grad.shape, BF16),
        ),
        "s" + "v" * 5,
        (
            first_flag,
            stage(spread, 0),
            score_grad,
            rewards[None],
            sample_group[None],
            head_sample,
        ),
    )
    first = stage(relay, 1).reshape(tp_count, rows_in, width)

    grad = incoming[0]
    query, kv, inverse, cos, sin, cos_t, sin_t, wkv = kernel_call(
        forward_body,
        (
            jax.ShapeDtypeStruct((ROWS, wq.shape[1]), BF16),
            jax.ShapeDtypeStruct((share, TICKS, 2 * kv_share, ROWS), BF16),
            jax.ShapeDtypeStruct((TICKS, ROWS, 1), F32),
            jax.ShapeDtypeStruct((ROWS, HD), F32),
            jax.ShapeDtypeStruct((ROWS, HD), F32),
            jax.ShapeDtypeStruct((TICKS, kv_share, ROWS), F32),
            jax.ShapeDtypeStruct((TICKS, kv_share, ROWS), F32),
            jax.ShapeDtypeStruct((2 * kv_share, wk.shape[1]), BF16),
        ),
        "ss" + "v" * 10,
        (place, odd, seg_lengths, wq, wk, wv, gain, *tables, first),
    )
    kv = lax.all_to_all(kv, "tp", 0, 0, axis_index_groups=groups)

    ready = []
    outputs = []
    for tick in range(TICKS):
        if tick == 0:
            got, got_at = first, TICKS * ROWS
        else:
            grad = received
            (packed,) = kernel_call(turn_body, blocks_of(ROWS), "v", (grad,))
            got, got_at = exchange(packed), 0
        dquery, dkv, along = kernel_call(
            functools.partial(attention_body, tick, got_at),
            (
                jax.ShapeDtypeStruct(query.shape, BF16),
                jax.ShapeDtypeStruct((share, 2 * kv_share, ROWS), BF16),
                jax.ShapeDtypeStruct((ROWS, 1), F32),
            ),
            "s" + "v" * (7 + len(ready)),
            (odd, seg_lengths, got, wo, query, kv, cos, sin, *ready),
        )
        dkv = lax.all_to_all(dkv, "tp", 0, 0, axis_index_groups=groups)
        (blocks,) = kernel_call(
            functools.partial(partial_body, tick),
            blocks_of(ROWS),
            "s" + "v" * 10,
            (odd, first, dquery, dkv, wq, wkv, gain, inverse, along, cos_t, sin_t),
        )
        blocks = exchange(blocks)
        if tick == 0:
            blocks, inverse = lax.optimization_barrier((blocks, inverse))
        total = jnp.sum(blocks.astype(F32), axis=0)
        result = (grad.astype(F32) + total).astype(BF16)
        received = ring_down(jnp.where(first_section, heads[tick], result), "pipe")
        if tick == 0:
            later = kernel_call(
                functools.partial(query_body, 1),
                (
                    jax.ShapeDtypeStruct(query.shape, BF16),
                    jax.ShapeDtypeStruct((query.shape[1] // HD, ROWS, ROWS), F32),
                    jax.ShapeDtypeStruct((ROWS, HD), F32),
                    jax.ShapeDtypeStruct((ROWS, HD), F32),
                ),
                "s" + "v" * 8,
                (odd, seg_lengths, wq, gain, first, kv, inverse, tables[0], tables[1]),
            )
            received, result, later = lax.optimization_barrier((received, result, later))
            query, *ready, cos, sin = later
        outputs.append(result)
    return (jnp.stack(outputs, axis=0)[None], received[None])


def solution(mesh):
    placed = (
        P("pipe", None, None, "tp"),
        P("pipe", None, "tp"),
        P("pipe", None),
        P("pipe", None, "tp"),
        P("pipe", None, "tp"),
        P("pipe", None, "tp"),
        P("pipe", "tp", None),
        P("pipe", None, None),
        P(None, None, "tp"),
        P(),
        P(),
        P(),
    )
    return jax.shard_map(
        per_device,
        mesh=mesh,
        in_specs=placed,
        out_specs=(P("pipe", None, None, "tp"), P("pipe", None, "tp")),
        check_vma=False,
    )
```
